256 devices in a mesh: wide: 64 (over y, z, x_lo), sub: 4 (over x_hi, core).
Axes of the slice: x: 4 (x_hi: 2, x_lo: 2; x = x_hi * 2 + x_lo), y: 4, z: 8, core: 2. Of those that a mesh axis runs over, the one named last changes fastest.
Arguments:
- embeddings: float32 [262144, 1024], P(('wide', 'sub')), may hold values from -40 to 40
- first_child: int32 [256], replicated, may hold values from 0 to 1024, as said below
- start_basis: float32 [512, 1024], replicated, may hold values from -0.1875 to 0.1875
Outputs:
- moved_rows: float32 [524288, 1024], P(('wide', 'sub'))
- basis: float32 [512, 1024], P('wide')
- factor: float32 [512, 64], P('wide')
The draws below stay inside these ranges and needn't reach their ends.
Inputs may be any that keep to these rules, and one draw needn't show every extreme that they name: `first_child`: in every cluster some partner pair has 1024 on both devices and another partner pair 0 on both.
All inputs are finite; a program needn't handle non-finite values.
Results may differ from the reference program's by a relative error of at most 0.0003.
Values sent between devices are 32-bit elements; how exact they have to be, the bound alone decides.
No kernel may reach another device: no remote copies, remote signals or barrier semaphores. Data moves between devices by JAX's collectives and lax.ppermute only.
A program may use at most 128 MiB of HBM per device.

```python
import math
import jax
import jax.numpy as jnp
from jax import lax

D = 1024
K = 64
STEPS = 2
ROWS_DEV = 1024
ROWS = 262144
CHILDREN = 8
HALF = 8
N_SUB = 4
DEVICES = 256


def draw_embeddings(key, part):
    key = jax.random.fold_in(key, 11)
    scale_key, offset_key, random_key = jax.random.split(key, 3)
    column_scale = jnp.exp(jax.random.uniform(scale_key, (D,), jnp.float32, 0.0, math.log(3.0)))
    offset_value = jax.random.normal(offset_key, (D,), jnp.float32)
    random_part = jax.random.normal(random_key, (ROWS, D), jnp.float32)
    return random_part * column_scale + offset_value


def draw_first_child(key, part):
    key = jax.random.fold_in(key, 5)
    count_key, choose_key = jax.random.split(key)
    counts = jax.random.randint(count_key, (DEVICES,), 0, ROWS_DEV + 1, dtype=jnp.int32)
    clusters = CHILDREN // 2
    pair_count = HALF * N_SUB
    layout = counts.reshape(clusters, 2, pair_count)
    chosen = jax.vmap(lambda single: jax.random.permutation(single, pair_count))(jax.random.split(choose_key, clusters))
    places = jnp.arange(pair_count, dtype=jnp.int32)[None, :]
    full_pair = (places == chosen[:, 0:1])[:, None, :]
    empty_pair = (places == chosen[:, 1:2])[:, None, :]
    layout = jnp.where(full_pair, ROWS_DEV, layout)
    layout = jnp.where(empty_pair, 0, layout)
    return layout.reshape(DEVICES).astype(jnp.int32)


def normal_values(rng, shape, deviation, most, kind=jnp.bfloat16):
    array = deviation * jax.random.normal(rng, shape, jnp.float32)
    return jnp.clip(array, min=-most, max=most).astype(kind)


def setup_inputs(seed: int = 0) -> dict:
    splits = jax.random.split(jax.random.key(seed), 4)
    embeddings = draw_embeddings(jax.random.fold_in(splits[3], 71), 0)
    first_child = draw_first_child(jax.random.fold_in(splits[3], 71), 0)
    start_basis = normal_values(splits[2], (CHILDREN * K, D), D ** -0.5, 0.1875, jnp.float32)
    return dict(embeddings=embeddings, first_child=first_child, start_basis=start_basis)


precise = lax.Precision.HIGHEST

def member_front(source_block, start_row, length):
    row_count = source_block.shape[0]
    doubled = jnp.concatenate([source_block, jnp.zeros_like(source_block)], axis=0)
    shifted = lax.dynamic_slice_in_dim(doubled, start_row, row_count, 0)
    inside = lax.iota(jnp.int32, row_count) < length
    return jnp.where(inside[:, None], shifted, jnp.zeros_like(shifted))

def member_buffer(own_block, other_block, own_start, own_length, other_start, other_length):
    row_count, feature_count = own_block.shape
    own_part = member_front(own_block, own_start, own_length)
    other_part = member_front(other_block, other_start, other_length)
    zero_rows = jnp.zeros((2 * row_count, feature_count), own_block.dtype)
    buffer = lax.dynamic_update_slice(zero_rows, own_part, (jnp.int32(0), jnp.int32(0)))
    placed = lax.dynamic_update_slice(zero_rows, other_part, (own_length.astype(jnp.int32), jnp.int32(0)))
    return buffer + placed

def centered(product_sums, current, member_mean, member_total):
    projected_mean = jnp.dot(current, member_mean, precision=precise)
    return (product_sums - member_total * projected_mean[:, None] * member_mean[None, :]) / member_total

def orthonormal(image_rows):
    gram_matrix = jnp.dot(image_rows, image_rows.T, precision=precise)
    lower_factor = jnp.linalg.cholesky(gram_matrix)
    vectors = jax.scipy.linalg.solve_triangular(lower_factor, image_rows, lower=True)
    return (vectors, lower_factor)

def cluster_basis(group_rows, group_first, pair_basis):
    position = jnp.arange(group_rows.shape[0], dtype=jnp.int32) % ROWS_DEV
    first_limit = jnp.repeat(group_first, ROWS_DEV)
    first_mask = (position < first_limit).astype(group_rows.dtype)
    member_masks = jnp.stack([first_mask, 1.0 - first_mask])
    member_counts = lax.optimization_barrier(jnp.sum(member_masks, axis=1))
    row_sums = jnp.dot(member_masks, group_rows, precision=precise)
    member_means = row_sums / member_counts[:, None]
    column_weights = jnp.repeat(member_masks, K, axis=0)
    current = pair_basis
    factors = pair_basis
    for sweep in range(STEPS):
        projected = lax.dot_general(current, group_rows, (((1,), (1,)), ((), ())), precision=precise)
        projected = projected * column_weights
        product_sums = jnp.dot(projected, group_rows, precision=precise)
        vector_list = []
        factor_list = []
        for member in range(2):
            image_rows = centered(product_sums[member * K:(member + 1) * K], current[member * K:(member + 1) * K], member_means[member], member_counts[member])
            vectors, lower_factor = orthonormal(image_rows)
            vector_list.append(vectors)
            factor_list.append(lower_factor)
        current = jnp.concatenate(vector_list, axis=0)
        factors = jnp.concatenate(factor_list, axis=0)
    return (current, factors)

def cluster_item(items):
    return cluster_basis(items[0], items[1], items[2])

def reference(embeddings, first_child, start_basis):
    blocks = embeddings.reshape(DEVICES, ROWS_DEV, D)
    every_index = jnp.arange(DEVICES, dtype=jnp.int32)

    def place_device(device_index):
        wide_pos = device_index // N_SUB
        sub_pos = device_index % N_SUB
        partner_index = jnp.bitwise_xor(wide_pos, HALF) * N_SUB + sub_pos
        upper_half = wide_pos // HALF % 2
        own_first = first_child[device_index]
        partner_first = first_child[partner_index]
        own_start = jnp.where(upper_half == 1, own_first, 0).astype(jnp.int32)
        own_length = jnp.where(upper_half == 1, ROWS_DEV - own_first, own_first).astype(jnp.int32)
        partner_start = jnp.where(upper_half == 1, partner_first, 0).astype(jnp.int32)
        partner_length = jnp.where(upper_half == 1, ROWS_DEV - partner_first, partner_first).astype(jnp.int32)
        return member_buffer(blocks[device_index], blocks[partner_index], own_start, own_length, partner_start, partner_length)
    moved_rows = lax.map(place_device, every_index).reshape(DEVICES * 2 * ROWS_DEV, D)
    clusters = CHILDREN // 2
    group_rows = embeddings.reshape(clusters, -1, D)
    group_first = first_child.reshape(clusters, -1)
    pair_basis = start_basis.reshape(clusters, 2 * K, D)
    vectors, factors = lax.map(cluster_item, (group_rows, group_first, pair_basis))
    basis = math.sqrt(D) * vectors.reshape(CHILDREN * K, D)
    return (moved_rows, basis, factors.reshape(CHILDREN * K, K))
```

```python
import functools
import math

import jax
import jax.numpy as jnp
import numpy as np
from jax import lax
from jax.experimental import pallas as pl
from jax.experimental.pallas import tpu as pltpu
from jax.sharding import Mesh, PartitionSpec as P

CHILDREN = 8
Y, Z, XL, XH, CORE = 4, 8, 2, 2, 2
AXES = ("y", "z", "xl", "xh", "core")
F32 = jnp.float32
VMEM_LIMIT = 40 * 1024 * 1024
PIECES = (128, 56, 64, 120, 80, 56, 64, 200)
TAIL_ROWS = 128
TAIL = 2
SENT = sum(PIECES)
CLUSTER, FLAT, PARTNER, CORE_AT, X_AT, UPPER, PIECE = range(7)


def split(values):
    high = values.astype(jnp.bfloat16)
    return high, (values - high.astype(F32)).astype(jnp.bfloat16)


def dot_split(left, right, dims):
    (lh, ll), (rh, rl) = left, right

    def dot(a, b):
        return lax.dot_general(a, b, (dims, ((), ())), preferred_element_type=F32)

    return dot(lh, rh) + (dot(lh, rl) + dot(ll, rh))


ROW_BY_ROW = ((1,), (1,))
PLAIN = ((1,), (0,))


def dot_precise(left, right, dims):
    return lax.dot_general(
        left, right, (dims, ((), ())), precision=lax.Precision.HIGHEST, preferred_element_type=F32
    )


def masked_products(vectors, rows, first, start, with_sums):
    count = rows.shape[0]
    rows_split = split(rows)
    projected = dot_split(split(vectors), rows_split, ROW_BY_ROW)
    position = start + lax.broadcasted_iota(jnp.int32, projected.shape, 1)
    child = lax.broadcasted_iota(jnp.int32, projected.shape, 0) // (vectors.shape[0] // 2)
    outside = (position >= first).astype(jnp.int32)
    projected = jnp.where(outside == child, projected, 0.0)
    if with_sums:
        position = start + lax.broadcasted_iota(jnp.int32, (8, count), 1)
        which = lax.broadcasted_iota(jnp.int32, (8, count), 0)
        inside = (position < first).astype(F32)
        members = jnp.where(which == 0, inside, jnp.where(which == 1, 1.0 - inside, 0.0))
        projected = jnp.concatenate([projected, members], axis=0)
    return dot_split(split(projected), rows_split, PLAIN)


def factorize(grams):
    size = grams[0].shape[0]
    lane = lax.broadcasted_iota(jnp.int32, (size, size), 1)
    row = lax.broadcasted_iota(jnp.int32, (size, size), 0)
    eye = (lane == row).astype(F32)
    tables = [
        [jnp.concatenate([g, eye], axis=1)[t * 8 : t * 8 + 8] for t in range(size // 8)] for g in grams
    ]
    sub = lax.broadcasted_iota(jnp.int32, (8, 2 * size), 0)
    for step in range(size):
        tile, place = divmod(step, 8)
        for table in tables:
            pivot_row = table[tile][place : place + 1]
            pivot = pivot_row[:, step : step + 1]
            scaled = pivot_row / jnp.broadcast_to(pivot, pivot_row.shape)
            for t in range(tile, size // 8):
                column = jnp.broadcast_to(table[t][:, step : step + 1], table[t].shape)
                if t == tile:
                    column = jnp.where(sub > place, column, 0.0)
                table[t] = table[t] - column * scaled
    results = []
    for table in tables:
        full = jnp.concatenate(table, axis=0)
        upper, lower_inverse = full[:, :size], full[:, size:]
        diagonal = jnp.sum(jnp.where(lane == row, upper, 0.0), axis=1, keepdims=True)
        scale = 1.0 / jnp.sqrt(diagonal)
        results.append((jnp.where(lane >= row, upper * scale, 0.0), lower_inverse * scale))
    return results


def image(sums, vectors, mean, total):
    high, low = split(vectors)
    projected_mean = jnp.sum((high.astype(F32) + low.astype(F32)) * mean, axis=1, keepdims=True)
    return (sums - total * projected_mean * mean) / total


def member_counts(info, first, rows):
    group = 2 * first.shape[0] // CHILDREN
    base = info[CLUSTER] * group
    total = lax.fori_loop(0, group, lambda i, t: t + first[base + i], jnp.int32(0))
    return total.astype(F32), (group * rows - total).astype(F32)


def spans(info, first, rows):
    own, partner, upper = first[info[FLAT]], first[info[PARTNER]], info[UPPER] == 1
    return (
        jnp.where(upper, own, 0), jnp.where(upper, rows - own, own),
        jnp.where(upper, partner, 0), jnp.where(upper, rows - partner, partner),
    )


def column_blocks(info):
    for r in range(4):
        for far, c in ((False, info[CORE_AT]), (True, 1 - info[CORE_AT])):
            yield r, far, pl.ds(pl.multiple_of((c * 4 + (info[X_AT] ^ r)) * 128, 128), 128)


def first_kernel(info, first, basis_ref, rows_ref, mine_ref, other_ref, total):
    step = pl.program_id(0)
    count = rows_ref.shape[0]

    @pl.when(step == 0)
    def _():
        total[...] = jnp.zeros_like(total)

    own_first = first[info[FLAT]]
    total[...] += masked_products(basis_ref[...], rows_ref[...], own_first, step * count, True)

    @pl.when(step == pl.num_programs(0) - 1)
    def _():
        for r, far, columns in column_blocks(info):
            (other_ref if far else mine_ref)[r] = total[:, columns]


def middle_kernel(
    info, first, own_ref, far_ref, basis_ref, rows_ref,
    mine_ref, other_ref, vectors_ref, mean_ref, total, current, later,
):
    step = pl.program_id(0)
    count = rows_ref.shape[0]
    k = basis_ref.shape[0] // 2
    upper = info[UPPER]

    @pl.when(step == 0)
    def _():
        for r, far, columns in column_blocks(info):
            total[:, columns] = (far_ref if far else own_ref)[r]
        counts = member_counts(info, first, pl.num_programs(0) * count)
        images, grams = [], []
        for c in range(2):
            mean = total[2 * k + c : 2 * k + c + 1, :] / counts[c]
            mean_ref[pl.ds(c, 1), :] = mean
            images.append(image(total[c * k : c * k + k, :], basis_ref[c * k : c * k + k, :], mean, counts[c]))
            grams.append(dot_precise(images[c], images[c], ROW_BY_ROW))
        for c, (_, inverse) in enumerate(factorize(grams)):
            current[c * k : c * k + k, :] = dot_precise(inverse, images[c], PLAIN)
        vectors_ref[...] = current[pl.ds(pl.multiple_of(upper * k, k), k), :]
        later[...] = jnp.zeros_like(later)

    own_first = first[info[FLAT]]
    later[...] += masked_products(current[...], rows_ref[...], own_first, step * count, False)

    @pl.when(step == pl.num_programs(0) - 1)
    def _():
        for r, far, columns in column_blocks(info):
            for n, half in enumerate((upper, 1 - upper)):
                ref = other_ref if far else mine_ref
                ref[r, n * k : n * k + k] = later[pl.ds(pl.multiple_of(half * k, k), k), columns]


def last_kernel(info, first, own_ref, far_ref, vectors_ref, mean_ref, basis_ref, factor_ref, total, lower, *, rows):
    for r, far, columns in column_blocks(info):
        total[:, columns] = (far_ref if far else own_ref)[r]
    counts = member_counts(info, first, rows)
    child = info[UPPER]
    mean = jnp.where(child == 0, mean_ref[0:1, :], mean_ref[1:2, :])
    count = jnp.where(child == 0, counts[0], counts[1])
    image_rows = image(total[...], vectors_ref[...], mean, count)
    gram = dot_precise(image_rows, image_rows, ROW_BY_ROW)
    ((transposed, inverse),) = factorize([gram])
    total[...] = dot_precise(inverse, image_rows, PLAIN)
    lower[...] = transposed.T
    start = pl.multiple_of(info[PIECE], 8)
    basis_ref[...] = math.sqrt(total.shape[1]) * total[pl.ds(start, 8), :]
    factor_ref[...] = lower[pl.ds(start, 8), :]


def add_kernel(left_ref, right_ref, *outs):
    for r, out in enumerate(outs):
        out[...] = left_ref[r] + right_ref[r]


def shifted_rows(ref, start, count):
    aligned = pl.multiple_of(start // 8 * 8, 8)
    window = ref[pl.ds(aligned, count + 8), :]
    return pltpu.roll(window, jnp.where(start == aligned, 0, count + 8 - (start - aligned)), 0)[:count]


def piece_base(info, at, size, rows):
    return pl.multiple_of(jnp.where(info[UPPER] == 1, rows - at - size, at), 8)


def place_kernel(info, first, own_ref, *refs):
    pieces, out_ref, own, other, sems = refs[:-4], refs[-4], refs[-3], refs[-2], refs[-1]
    step = pl.program_id(0)
    count = out_ref.shape[0]
    rows = own_ref.shape[0]
    copies = [pltpu.make_async_copy(own_ref, own.at[pl.ds(0, rows)], sems.at[0])]
    at = 0
    for n, piece in enumerate(pieces):
        size = piece.shape[0]
        target = other.at[pl.ds(count + piece_base(info, at, size, rows), size)]
        copies.append(pltpu.make_async_copy(piece, target, sems.at[n + 1]))
        at += size

    @pl.when(step == 0)
    def _():
        for copy in copies:
            copy.start()
        for copy in copies:
            copy.wait()

    own_start, own_length, start, length = spans(info, first, rows)
    base = step * count
    place = base + lax.broadcasted_iota(jnp.int32, out_ref.shape, 0)
    own_rows = shifted_rows(own, jnp.minimum(own_start + base, rows), count)
    other_from = jnp.clip(base - own_length + start + count, 0, rows + count)
    other_rows = shifted_rows(other, other_from, count)
    there = place - own_length + start
    sent_from = jnp.where(info[UPPER] == 1, rows - SENT, 0)
    arrived = (there >= jnp.maximum(start, sent_from)) & (there < jnp.minimum(start + length, sent_from + SENT))
    out_ref[...] = jnp.where(place < own_length, own_rows, jnp.where(arrived, other_rows, 0.0))


def tail_kernel(info, first, piece_ref, moved_ref, out_ref, piece, window, edges, sems, *, at, rows):
    del moved_ref
    size = piece_ref.shape[0]
    _, own_length, start, length = spans(info, first, rows)
    base = piece_base(info, at, size, rows)
    low = jnp.maximum(base, start)
    count = jnp.minimum(base + size, start + length) - low
    target = own_length + low - start

    @pl.when(count > 0)
    def _():
        aligned = pl.multiple_of(target // 8 * 8, 8)
        skip = target - aligned
        tiles = (skip + count + 7) // 8
        tail = pl.multiple_of((tiles - 1) * 8, 8)
        loads = [
            pltpu.make_async_copy(piece_ref, piece.at[pl.ds(8, size)], sems.at[0]),
            pltpu.make_async_copy(out_ref.at[pl.ds(aligned, 8)], edges.at[pl.ds(0, 8)], sems.at[1]),
            pltpu.make_async_copy(out_ref.at[pl.ds(aligned + tail, 8)], edges.at[pl.ds(8, 8)], sems.at[2]),
        ]
        for load in loads:
            load.start()
        for load in loads:
            load.wait()
        rows_in = window.shape[0]
        window[...] = shifted_rows(piece, low - base - skip + 8, rows_in)
        row = lax.broadcasted_iota(jnp.int32, (8, window.shape[1]), 0)
        window[0:8] = jnp.where(row < skip, edges[0:8], window[0:8])
        kept = window[pl.ds(tail, 8), :]
        window[pl.ds(tail, 8), :] = jnp.where(row + tail < skip + count, kept, edges[8:16])

        def store(tile):
            at_row = pl.multiple_of(tile * 8, 8)
            return pltpu.make_async_copy(
                window.at[pl.ds(at_row, 8)], out_ref.at[pl.ds(pl.multiple_of(aligned + at_row, 8), 8)], sems.at[3 + tile]
            )

        @pl.loop(0, tiles)
        def _(tile):
            store(tile).start()

        @pl.loop(0, tiles)
        def _(tile):
            store(tile).wait()


def flip(values, axis, bits):
    size = 4 if axis == ("xl", "xh") else {"z": Z, "core": CORE}[axis]
    return lax.ppermute(values, axis, [(i, i ^ bits) for i in range(size)])


def flip_x(values, r):
    return flip(values, ("xl", "xh"), (r & 1) * 2 + (r >> 1))


def params():
    return pltpu.CompilerParams(vmem_limit_bytes=VMEM_LIMIT)


def cheap():
    return pl.CostEstimate(flops=1024, bytes_accessed=1024, transcendentals=0)


VMEM = pl.BlockSpec(memory_space=pltpu.VMEM)
ANY = pl.BlockSpec(memory_space=pl.ANY)


def shape(*dims):
    return jax.ShapeDtypeStruct(dims, F32)


def whole(*dims):
    return pl.BlockSpec(dims, lambda i, info, first: (0,) * len(dims))


def call(kernel, name, grid, in_specs, out_specs, out_shape, scratch=(), aliases=None):
    return pl.pallas_call(
        kernel,
        grid_spec=pltpu.PrefetchScalarGridSpec(
            num_scalar_prefetch=2, grid=grid, in_specs=in_specs, out_specs=out_specs, scratch_shapes=scratch
        ),
        out_shape=out_shape,
        input_output_aliases=aliases or {},
        compiler_params=params(),
        cost_estimate=cheap(),
        name=name,
    )


def add_pieces(left, right):
    n = left.shape[0]
    return pl.pallas_call(
        add_kernel, out_shape=[shape(*left.shape[1:])] * n, in_specs=[VMEM, VMEM], out_specs=[VMEM] * n,
        cost_estimate=cheap(), name="add_pieces",
    )(left, right)


def table_of_places():
    flat = np.arange(Y * Z * XL * XH * CORE)
    core, xh, xl, z, y = flat % 2, flat // 2 % 2, flat // 4 % 2, flat // 8 % Z, flat // (8 * Z)
    half = (Z // 2) * XL * XH * CORE
    piece = (z % (Z // 2) * XL + xl) * 8
    columns = [y, flat, flat ^ half, core, xh * 2 + xl, z // (Z // 2), piece, 0 * flat]
    return np.stack(columns, axis=1).astype(np.int32)


def body(embeddings, first_child, start_basis):
    rows, features = embeddings.shape
    k = start_basis.shape[0] // CHILDREN
    flat = lax.axis_index(AXES)
    info = lax.dynamic_slice_in_dim(jnp.asarray(table_of_places()), flat, 1, 0).reshape(-1)
    upper = lax.axis_index("z") // (Z // 2)
    barrier = lax.optimization_barrier

    edges = [sum(PIECES[:n]) for n in range(len(PIECES) + 1)]
    arrived = []

    def send(at, size, pairs, source):
        start = jnp.where(upper == 1, at, rows - at - size)
        return lax.ppermute(lax.dynamic_slice_in_dim(source, start, size, 0), "z", pairs)

    both = [(i, i ^ (Z // 2)) for i in range(Z)]

    def start_piece(after):
        n = len(arrived)
        source, _ = barrier((embeddings, after))
        arrived.append(send(edges[n], PIECES[n], both, source))

    def end_piece(n, *values):
        *values, arrived[n] = barrier((*values, arrived[n]))
        return values[0] if len(values) == 1 else values

    block = 256
    grid = (rows // block,)
    row_block = pl.BlockSpec((block, features), lambda i, info, first: (i, 0))
    basis_block = pl.BlockSpec((2 * k, features), lambda i, info, first: (info[0], 0))

    start_piece(upper)
    mine, other = call(
        first_kernel, "first_products", grid, [basis_block, row_block],
        [whole(4, 2 * k + 8, 128)] * 2, [shape(4, 2 * k + 8, 128)] * 2, [pltpu.VMEM((2 * k + 8, features), F32)],
    )(info, first_child, start_basis, embeddings)

    def scatter_x(parts):
        return parts[0] + flip_x(parts[1], 1) + flip_x(parts[2], 2) + flip_x(parts[3], 3)

    def gather_x(total):
        return jnp.stack([total] + [flip_x(total, r) for r in (1, 2, 3)])

    total = end_piece(0, scatter_x(add_pieces(mine, flip(other, "core", 1))))
    start_piece(total)
    total = total + flip(total, "z", 4)
    total = end_piece(1, total + flip(total, "z", 2))
    start_piece(total)
    total = total + flip(total, "z", 1)
    own = end_piece(2, gather_x(total))
    start_piece(own)
    far = flip(own, "core", 1)
    mine, other, vectors, mean = call(
        middle_kernel, "middle", grid,
        [whole(4, 2 * k + 8, 128), whole(4, 2 * k + 8, 128), basis_block, row_block],
        [whole(4, 2 * k, 128), whole(4, 2 * k, 128), whole(k, features), whole(8, features)],
        [shape(4, 2 * k, 128)] * 2 + [shape(k, features), shape(8, features)],
        [pltpu.VMEM((2 * k + 8, features), F32), pltpu.VMEM((2 * k, features), F32), pltpu.VMEM((2 * k, features), F32)],
    )(info, first_child, own, far, start_basis, embeddings)

    mine, other = end_piece(3, mine, other)
    start_piece(mine)
    total = end_piece(4, scatter_x(add_pieces(mine, flip(other, "core", 1))))
    start_piece(total)
    kept = total[:k] + flip(total[k:], "z", 4)
    kept = end_piece(5, kept + flip(kept, "z", 2))
    start_piece(kept)
    kept = kept + flip(kept, "z", 1)
    own = end_piece(6, gather_x(kept))
    start_piece(own)
    far = flip(own, "core", 1)
    basis, factor = call(
        functools.partial(last_kernel, rows=rows), "last", (1,),
        [whole(4, k, 128), whole(4, k, 128), whole(k, features), whole(8, features)],
        [whole(8, features), whole(8, k)], [shape(8, features), shape(8, k)],
        [pltpu.VMEM((k, features), F32), pltpu.VMEM((k, k), F32)],
    )(info, first_child, own, far, vectors, mean)
    basis, factor = end_piece(7, basis, factor)

    out_block = 256

    def place(source, arrived):
        return call(
            place_kernel, "place", (2 * rows // out_block,), [ANY] * (1 + len(PIECES)),
            pl.BlockSpec((out_block, features), lambda i, info, first: (i, 0)), shape(2 * rows, features),
            [
                pltpu.VMEM((rows + out_block + 8, features), F32),
                pltpu.VMEM((rows + 2 * out_block + 8, features), F32),
                pltpu.SemaphoreType.DMA((1 + len(PIECES),)),
            ],
        )(info, first_child, source, *arrived)

    def place_tail(moved, piece, at):
        window = TAIL_ROWS + 16
        return call(
            functools.partial(tail_kernel, at=at, rows=rows), "place_tail", (1,), [ANY, ANY], ANY,
            shape(2 * rows, features),
            [
                pltpu.VMEM((TAIL_ROWS + 8 + window + 8, features), F32), pltpu.VMEM((window, features), F32),
                pltpu.VMEM((16, features), F32), pltpu.SemaphoreType.DMA((3 + window // 8,)),
            ],
            {3: 0},
        )(info, first_child, piece, moved)

    half = Z // 2

    def finish(up, down):
        def branch(source, *arrived):
            pieces = []
            for n in range(max(up, down)):
                pairs = [(i, i + half) for i in range(half) if n < up] + [(i + half, i) for i in range(half) if n < down]
                at = SENT + n * TAIL_ROWS
                pieces.append((send(at, TAIL_ROWS, pairs, source), at))
            moved = place(source, arrived)
            for piece, at in pieces:
                moved = place_tail(moved, piece, at)
            return moved

        return branch

    def tail_pieces(needed):
        return (jnp.maximum(needed - SENT, 0) + TAIL_ROWS - 1) // TAIL_ROWS

    own_first, partner_first = first_child[flat], first_child[jnp.bitwise_xor(flat, half * XL * XH * CORE)]
    up = tail_pieces(rows - jnp.where(upper == 1, partner_first, own_first))
    down = tail_pieces(jnp.where(upper == 1, own_first, partner_first))
    branches = [finish(a, b) for a in range(TAIL + 1) for b in range(TAIL + 1)]
    moved_rows = lax.switch(up * (TAIL + 1) + down, branches, embeddings, *arrived)
    return moved_rows, basis, factor


def solution(mesh):
    fine = Mesh(mesh.devices.reshape(Y, Z, XL, XH, CORE), AXES)
    return jax.shard_map(
        body,
        mesh=fine,
        in_specs=(P(AXES, None), P(), P()),
        out_specs=(P(AXES, None), P(("y", "z", "xl"), None), P(("y", "z", "xl"), None)),
        check_vma=False,
    )
```

```python
import functools
import math

import jax
import jax.numpy as jnp
import numpy as np
from jax import lax
from jax.experimental import pallas as pl
from jax.experimental.pallas import tpu as pltpu
from jax.sharding import Mesh, PartitionSpec as P

CHILDREN = 8
Y, Z, XL, XH, CORE = 4, 8, 2, 2, 2
AXES = ("y", "z", "xl", "xh", "core")
F32 = jnp.float32
VMEM_LIMIT = 40 * 1024 * 1024
PIECES = (360, 184, 72, 152)
TAIL_ROWS = 128
TAIL = 2
SENT = sum(PIECES)
CLUSTER, FLAT, PARTNER, CORE_AT, X_AT, UPPER, PIECE = range(7)


def split(values):
    high = values.astype(jnp.bfloat16)
    return high, (values - high.astype(F32)).astype(jnp.bfloat16)


def dot_split(left, right, dims):
    (lh, ll), (rh, rl) = left, right

    def dot(a, b):
        return lax.dot_general(a, b, (dims, ((), ())), preferred_element_type=F32)

    return dot(lh, rh) + (dot(lh, rl) + dot(ll, rh))


ROW_BY_ROW = ((1,), (1,))
PLAIN = ((1,), (0,))


def dot_precise(left, right, dims):
    return lax.dot_general(
        left, right, (dims, ((), ())), precision=lax.Precision.HIGHEST, preferred_element_type=F32
    )


def masked_products(vectors, rows, first, start, with_sums):
    count = rows.shape[0]
    rows_split = split(rows)
    projected = dot_split(split(vectors), rows_split, ROW_BY_ROW)
    position = start + lax.broadcasted_iota(jnp.int32, projected.shape, 1)
    child = lax.broadcasted_iota(jnp.int32, projected.shape, 0) // (vectors.shape[0] // 2)
    outside = (position >= first).astype(jnp.int32)
    projected = jnp.where(outside == child, projected, 0.0)
    if with_sums:
        position = start + lax.broadcasted_iota(jnp.int32, (8, count), 1)
        which = lax.broadcasted_iota(jnp.int32, (8, count), 0)
        inside = (position < first).astype(F32)
        members = jnp.where(which == 0, inside, jnp.where(which == 1, 1.0 - inside, 0.0))
        projected = jnp.concatenate([projected, members], axis=0)
    return dot_split(split(projected), rows_split, PLAIN)


def factorize(grams):
    size = grams[0].shape[0]
    lane = lax.broadcasted_iota(jnp.int32, (size, size), 1)
    row = lax.broadcasted_iota(jnp.int32, (size, size), 0)
    eye = (lane == row).astype(F32)
    tables = [
        [jnp.concatenate([g, eye], axis=1)[t * 8 : t * 8 + 8] for t in range(size // 8)] for g in grams
    ]
    sub = lax.broadcasted_iota(jnp.int32, (8, 2 * size), 0)
    for step in range(size):
        tile, place = divmod(step, 8)
        for table in tables:
            pivot_row = table[tile][place : place + 1]
            pivot = pivot_row[:, step : step + 1]
            scaled = pivot_row / jnp.broadcast_to(pivot, pivot_row.shape)
            for t in range(tile, size // 8):
                column = jnp.broadcast_to(table[t][:, step : step + 1], table[t].shape)
                if t == tile:
                    column = jnp.where(sub > place, column, 0.0)
                table[t] = table[t] - column * scaled
    results = []
    for table in tables:
        full = jnp.concatenate(table, axis=0)
        upper, lower_inverse = full[:, :size], full[:, size:]
        diagonal = jnp.sum(jnp.where(lane == row, upper, 0.0), axis=1, keepdims=True)
        scale = 1.0 / jnp.sqrt(diagonal)
        results.append((jnp.where(lane >= row, upper * scale, 0.0), lower_inverse * scale))
    return results


def image(sums, vectors, mean, total):
    high, low = split(vectors)
    projected_mean = jnp.sum((high.astype(F32) + low.astype(F32)) * mean, axis=1, keepdims=True)
    return (sums - total * projected_mean * mean) / total


def member_counts(info, first, rows):
    group = 2 * first.shape[0] // CHILDREN
    base = info[CLUSTER] * group
    total = lax.fori_loop(0, group, lambda i, t: t + first[base + i], jnp.int32(0))
    return total.astype(F32), (group * rows - total).astype(F32)


def spans(info, first, rows):
    own, partner, upper = first[info[FLAT]], first[info[PARTNER]], info[UPPER] == 1
    return (
        jnp.where(upper, own, 0), jnp.where(upper, rows - own, own),
        jnp.where(upper, partner, 0), jnp.where(upper, rows - partner, partner),
    )


def column_blocks(info):
    for r in range(4):
        for far, c in ((False, info[CORE_AT]), (True, 1 - info[CORE_AT])):
            yield r, far, pl.ds(pl.multiple_of((c * 4 + (info[X_AT] ^ r)) * 128, 128), 128)


def first_kernel(info, first, basis_ref, rows_ref, mine_ref, other_ref, total):
    step = pl.program_id(0)
    count = rows_ref.shape[0]

    @pl.when(step == 0)
    def _():
        total[...] = jnp.zeros_like(total)

    own_first = first[info[FLAT]]
    total[...] += masked_products(basis_ref[...], rows_ref[...], own_first, step * count, True)

    @pl.when(step == pl.num_programs(0) - 1)
    def _():
        for r, far, columns in column_blocks(info):
            (other_ref if far else mine_ref)[r] = total[:, columns]


def middle_kernel(
    info, first, own_ref, far_ref, basis_ref, rows_ref,
    mine_ref, other_ref, vectors_ref, mean_ref, total, current, later,
):
    step = pl.program_id(0)
    count = rows_ref.shape[0]
    k = basis_ref.shape[0] // 2
    upper = info[UPPER]

    @pl.when(step == 0)
    def _():
        for r, far, columns in column_blocks(info):
            total[:, columns] = (far_ref if far else own_ref)[r]
        counts = member_counts(info, first, pl.num_programs(0) * count)
        images, grams = [], []
        for c in range(2):
            mean = total[2 * k + c : 2 * k + c + 1, :] / counts[c]
            mean_ref[pl.ds(c, 1), :] = mean
            images.append(image(total[c * k : c * k + k, :], basis_ref[c * k : c * k + k, :], mean, counts[c]))
            grams.append(dot_precise(images[c], images[c], ROW_BY_ROW))
        for c, (_, inverse) in enumerate(factorize(grams)):
            current[c * k : c * k + k, :] = dot_precise(inverse, images[c], PLAIN)
        vectors_ref[...] = current[pl.ds(pl.multiple_of(upper * k, k), k), :]
        later[...] = jnp.zeros_like(later)

    own_first = first[info[FLAT]]
    later[...] += masked_products(current[...], rows_ref[...], own_first, step * count, False)

    @pl.when(step == pl.num_programs(0) - 1)
    def _():
        for r, far, columns in column_blocks(info):
            for n, half in enumerate((upper, 1 - upper)):
                ref = other_ref if far else mine_ref
                ref[r, n * k : n * k + k] = later[pl.ds(pl.multiple_of(half * k, k), k), columns]


def last_kernel(info, first, own_ref, far_ref, vectors_ref, mean_ref, basis_ref, factor_ref, total, lower, *, rows):
    for r, far, columns in column_blocks(info):
        total[:, columns] = (far_ref if far else own_ref)[r]
    counts = member_counts(info, first, rows)
    child = info[UPPER]
    mean = jnp.where(child == 0, mean_ref[0:1, :], mean_ref[1:2, :])
    count = jnp.where(child == 0, counts[0], counts[1])
    image_rows = image(total[...], vectors_ref[...], mean, count)
    gram = dot_precise(image_rows, image_rows, ROW_BY_ROW)
    ((transposed, inverse),) = factorize([gram])
    total[...] = dot_precise(inverse, image_rows, PLAIN)
    lower[...] = transposed.T
    start = pl.multiple_of(info[PIECE], 8)
    basis_ref[...] = math.sqrt(total.shape[1]) * total[pl.ds(start, 8), :]
    factor_ref[...] = lower[pl.ds(start, 8), :]


def add_kernel(left_ref, right_ref, *outs):
    for r, out in enumerate(outs):
        out[...] = left_ref[r] + right_ref[r]


def shifted_rows(ref, start, count):
    aligned = pl.multiple_of(start // 8 * 8, 8)
    window = ref[pl.ds(aligned, count + 8), :]
    return pltpu.roll(window, jnp.where(start == aligned, 0, count + 8 - (start - aligned)), 0)[:count]


def piece_base(info, at, size, rows):
    return pl.multiple_of(jnp.where(info[UPPER] == 1, rows - at - size, at), 8)


def place_kernel(info, first, own_ref, *refs):
    pieces, out_ref, own, other, sems = refs[:-4], refs[-4], refs[-3], refs[-2], refs[-1]
    step = pl.program_id(0)
    count = out_ref.shape[0]
    rows = own_ref.shape[0]
    copies = [pltpu.make_async_copy(own_ref, own.at[pl.ds(0, rows)], sems.at[0])]
    at = 0
    for n, piece in enumerate(pieces):
        size = piece.shape[0]
        target = other.at[pl.ds(count + piece_base(info, at, size, rows), size)]
        copies.append(pltpu.make_async_copy(piece, target, sems.at[n + 1]))
        at += size

    @pl.when(step == 0)
    def _():
        for copy in copies:
            copy.start()
        for copy in copies:
            copy.wait()

    own_start, own_length, start, length = spans(info, first, rows)
    base = step * count
    place = base + lax.broadcasted_iota(jnp.int32, out_ref.shape, 0)
    own_rows = shifted_rows(own, jnp.minimum(own_start + base, rows), count)
    other_from = jnp.clip(base - own_length + start + count, 0, rows + count)
    other_rows = shifted_rows(other, other_from, count)
    there = place - own_length + start
    sent_from = jnp.where(info[UPPER] == 1, rows - SENT, 0)
    arrived = (there >= jnp.maximum(start, sent_from)) & (there < jnp.minimum(start + length, sent_from + SENT))
    out_ref[...] = jnp.where(place < own_length, own_rows, jnp.where(arrived, other_rows, 0.0))


def tail_kernel(info, first, piece_ref, moved_ref, out_ref, piece, window, edges, sems, *, at, rows):
    del moved_ref
    size = piece_ref.shape[0]
    _, own_length, start, length = spans(info, first, rows)
    base = piece_base(info, at, size, rows)
    low = jnp.maximum(base, start)
    count = jnp.minimum(base + size, start + length) - low
    target = own_length + low - start

    @pl.when(count > 0)
    def _():
        aligned = pl.multiple_of(target // 8 * 8, 8)
        skip = target - aligned
        tiles = (skip + count + 7) // 8
        tail = pl.multiple_of((tiles - 1) * 8, 8)
        loads = [
            pltpu.make_async_copy(piece_ref, piece.at[pl.ds(8, size)], sems.at[0]),
            pltpu.make_async_copy(out_ref.at[pl.ds(aligned, 8)], edges.at[pl.ds(0, 8)], sems.at[1]),
            pltpu.make_async_copy(out_ref.at[pl.ds(aligned + tail, 8)], edges.at[pl.ds(8, 8)], sems.at[2]),
        ]
        for load in loads:
            load.start()
        for load in loads:
            load.wait()
        rows_in = window.shape[0]
        window[...] = shifted_rows(piece, low - base - skip + 8, rows_in)
        row = lax.broadcasted_iota(jnp.int32, (8, window.shape[1]), 0)
        window[0:8] = jnp.where(row < skip, edges[0:8], window[0:8])
        kept = window[pl.ds(tail, 8), :]
        window[pl.ds(tail, 8), :] = jnp.where(row + tail < skip + count, kept, edges[8:16])

        def store(tile):
            at_row = pl.multiple_of(tile * 8, 8)
            return pltpu.make_async_copy(
                window.at[pl.ds(at_row, 8)], out_ref.at[pl.ds(pl.multiple_of(aligned + at_row, 8), 8)], sems.at[3 + tile]
            )

        @pl.loop(0, tiles)
        def _(tile):
            store(tile).start()

        @pl.loop(0, tiles)
        def _(tile):
            store(tile).wait()


def flip(values, axis, bits):
    size = 4 if axis == ("xl", "xh") else {"z": Z, "core": CORE}[axis]
    return lax.ppermute(values, axis, [(i, i ^ bits) for i in range(size)])


def flip_x(values, r):
    return flip(values, ("xl", "xh"), (r & 1) * 2 + (r >> 1))


def params():
    return pltpu.CompilerParams(vmem_limit_bytes=VMEM_LIMIT)


def cheap():
    return pl.CostEstimate(flops=1024, bytes_accessed=1024, transcendentals=0)


VMEM = pl.BlockSpec(memory_space=pltpu.VMEM)
ANY = pl.BlockSpec(memory_space=pl.ANY)


def shape(*dims):
    return jax.ShapeDtypeStruct(dims, F32)


def whole(*dims):
    return pl.BlockSpec(dims, lambda i, info, first: (0,) * len(dims))


def call(kernel, name, grid, in_specs, out_specs, out_shape, scratch=(), aliases=None):
    return pl.pallas_call(
        kernel,
        grid_spec=pltpu.PrefetchScalarGridSpec(
            num_scalar_prefetch=2, grid=grid, in_specs=in_specs, out_specs=out_specs, scratch_shapes=scratch
        ),
        out_shape=out_shape,
        input_output_aliases=aliases or {},
        compiler_params=params(),
        cost_estimate=cheap(),
        name=name,
    )


def add_pieces(left, right):
    n = left.shape[0]
    return pl.pallas_call(
        add_kernel, out_shape=[shape(*left.shape[1:])] * n, in_specs=[VMEM, VMEM], out_specs=[VMEM] * n,
        cost_estimate=cheap(), name="add_pieces",
    )(left, right)


def table_of_places():
    flat = np.arange(Y * Z * XL * XH * CORE)
    core, xh, xl, z, y = flat % 2, flat // 2 % 2, flat // 4 % 2, flat // 8 % Z, flat // (8 * Z)
    half = (Z // 2) * XL * XH * CORE
    piece = (z % (Z // 2) * XL + xl) * 8
    columns = [y, flat, flat ^ half, core, xh * 2 + xl, z // (Z // 2), piece, 0 * flat]
    return np.stack(columns, axis=1).astype(np.int32)


def body(embeddings, first_child, start_basis):
    rows, features = embeddings.shape
    k = start_basis.shape[0] // CHILDREN
    flat = lax.axis_index(AXES)
    info = lax.dynamic_slice_in_dim(jnp.asarray(table_of_places()), flat, 1, 0).reshape(-1)
    upper = lax.axis_index("z") // (Z // 2)
    barrier = lax.optimization_barrier

    edges = [sum(PIECES[:n]) for n in range(len(PIECES) + 1)]
    arrived = []

    def piece_of(source, at, size):
        start = jnp.where(upper == 1, at, rows - at - size)
        return lax.dynamic_slice_in_dim(source, start, size, 0)

    tails = [piece_of(embeddings, SENT + n * TAIL_ROWS, TAIL_ROWS) for n in range(TAIL)]
    pieces = [piece_of(embeddings, a, b - a) for a, b in zip(edges[:-1], edges[1:])]

    def start_piece(after):
        piece, _ = barrier((pieces[len(arrived)], after))
        arrived.append(flip(piece, "z", Z // 2))

    def end_piece(n, *values):
        *values, arrived[n] = barrier((*values, arrived[n]))
        return values[0] if len(values) == 1 else values

    block = 256
    grid = (rows // block,)
    row_block = pl.BlockSpec((block, features), lambda i, info, first: (i, 0))
    basis_block = pl.BlockSpec((2 * k, features), lambda i, info, first: (info[0], 0))

    arrived.append(flip(pieces[0], "z", Z // 2))
    mine, other = call(
        first_kernel, "first_products", grid, [basis_block, row_block],
        [whole(4, 2 * k + 8, 128)] * 2, [shape(4, 2 * k + 8, 128)] * 2, [pltpu.VMEM((2 * k + 8, features), F32)],
    )(info, first_child, start_basis, embeddings)

    def scatter_x(parts):
        return parts[0] + flip_x(parts[1], 1) + flip_x(parts[2], 2) + flip_x(parts[3], 3)

    def sum_quad(total):
        return (total + flip(total, "z", 1)) + (flip(total, "z", 2) + flip(total, "z", 3))

    def gather_x(total):
        return jnp.stack([total] + [flip_x(total, r) for r in (1, 2, 3)])

    mine, other, pieces[1:], tails = barrier((mine, other, pieces[1:], tails))
    total = scatter_x(add_pieces(mine, flip(other, "core", 1)))
    total = end_piece(0, total + flip(total, "z", 4))
    total = sum_quad(total)
    start_piece(total)
    own = gather_x(total)
    far = flip(own, "core", 1)
    start_piece(far)
    mine, other, vectors, mean = call(
        middle_kernel, "middle", grid,
        [whole(4, 2 * k + 8, 128), whole(4, 2 * k + 8, 128), basis_block, row_block],
        [whole(4, 2 * k, 128), whole(4, 2 * k, 128), whole(k, features), whole(8, features)],
        [shape(4, 2 * k, 128)] * 2 + [shape(k, features), shape(8, features)],
        [pltpu.VMEM((2 * k + 8, features), F32), pltpu.VMEM((2 * k, features), F32), pltpu.VMEM((2 * k, features), F32)],
    )(info, first_child, own, far, start_basis, embeddings)

    mine, other = end_piece(1, mine, other)
    parts = add_pieces(mine, flip(other, "core", 1))
    total = scatter_x([end_piece(2, parts[0]), *parts[1:]])
    kept = total[:k] + flip(total[k:], "z", 4)
    kept = sum_quad(kept)
    start_piece(kept)
    own = gather_x(kept)
    far = flip(own, "core", 1)
    basis, factor = call(
        functools.partial(last_kernel, rows=rows), "last", (1,),
        [whole(4, k, 128), whole(4, k, 128), whole(k, features), whole(8, features)],
        [whole(8, features), whole(8, k)], [shape(8, features), shape(8, k)],
        [pltpu.VMEM((k, features), F32), pltpu.VMEM((k, k), F32)],
    )(info, first_child, own, far, vectors, mean)
    basis, factor = end_piece(3, basis, factor)

    out_block = 256

    def place(source, arrived):
        return call(
            place_kernel, "place", (2 * rows // out_block,), [ANY] * (1 + len(PIECES)),
            pl.BlockSpec((out_block, features), lambda i, info, first: (i, 0)), shape(2 * rows, features),
            [
                pltpu.VMEM((rows + out_block + 8, features), F32),
                pltpu.VMEM((rows + 2 * out_block + 8, features), F32),
                pltpu.SemaphoreType.DMA((1 + len(PIECES),)),
            ],
        )(info, first_child, source, *arrived)

    def place_tail(moved, piece, at):
        window = TAIL_ROWS + 16
        return call(
            functools.partial(tail_kernel, at=at, rows=rows), "place_tail", (1,), [ANY, ANY], ANY,
            shape(2 * rows, features),
            [
                pltpu.VMEM((TAIL_ROWS + 8 + window + 8, features), F32), pltpu.VMEM((window, features), F32),
                pltpu.VMEM((16, features), F32), pltpu.SemaphoreType.DMA((3 + window // 8,)),
            ],
            {3: 0},
        )(info, first_child, piece, moved)

    half = Z // 2

    def finish(up, down):
        def branch(source, tails, *arrived):
            pieces = []
            for n in range(max(up, down)):
                pairs = [(i, i + half) for i in range(half) if n < up] + [(i + half, i) for i in range(half) if n < down]
                at = SENT + n * TAIL_ROWS
                pieces.append((lax.ppermute(tails[n], "z", pairs), at))
            moved = place(source, arrived)
            for piece, at in pieces:
                moved = place_tail(moved, piece, at)
            return moved

        return branch

    def tail_pieces(needed):
        return (jnp.maximum(needed - SENT, 0) + TAIL_ROWS - 1) // TAIL_ROWS

    own_first, partner_first = first_child[flat], first_child[jnp.bitwise_xor(flat, half * XL * XH * CORE)]
    up = tail_pieces(rows - jnp.where(upper == 1, partner_first, own_first))
    down = tail_pieces(jnp.where(upper == 1, own_first, partner_first))
    branches = [finish(a, b) for a in range(TAIL + 1) for b in range(TAIL + 1)]
    moved_rows = lax.switch(up * (TAIL + 1) + down, branches, embeddings, tails, *arrived)
    return moved_rows, basis, factor


def solution(mesh):
    fine = Mesh(mesh.devices.reshape(Y, Z, XL, XH, CORE), AXES)
    return jax.shard_map(
        body,
        mesh=fine,
        in_specs=(P(AXES, None), P(), P()),
        out_specs=(P(AXES, None), P(("y", "z", "xl"), None), P(("y", "z", "xl"), None)),
        check_vma=False,
    )
```

```python
import functools
import math

import jax
import jax.numpy as jnp
import numpy as np
from jax import lax
from jax.experimental import pallas as pl
from jax.experimental.pallas import tpu as pltpu
from jax.sharding import Mesh, PartitionSpec as P

CHILDREN = 8
Y, Z, XL, XH, CORE = 4, 8, 2, 2, 2
AXES = ("y", "z", "xl", "xh", "core")
F32 = jnp.float32
VMEM_LIMIT = 40 * 1024 * 1024
PIECES = (264, 352, 152)
TAIL_ROWS = 128
TAIL = 2
SENT = sum(PIECES)
CLUSTER, FLAT, PARTNER, CORE_AT, X_AT, UPPER, PIECE = range(7)


def split(values):
    high = values.astype(jnp.bfloat16)
    return high, (values - high.astype(F32)).astype(jnp.bfloat16)


def dot_split(left, right, dims):
    (lh, ll), (rh, rl) = left, right

    def dot(a, b):
        return lax.dot_general(a, b, (dims, ((), ())), preferred_element_type=F32)

    return dot(lh, rh) + (dot(lh, rl) + dot(ll, rh))


ROW_BY_ROW = ((1,), (1,))
PLAIN = ((1,), (0,))


def dot_precise(left, right, dims):
    return lax.dot_general(
        left, right, (dims, ((), ())), precision=lax.Precision.HIGHEST, preferred_element_type=F32
    )


def masked_products(vectors, rows, first, start, with_sums):
    count = rows.shape[0]
    rows_split = split(rows)
    projected = dot_split(split(vectors), rows_split, ROW_BY_ROW)
    position = start + lax.broadcasted_iota(jnp.int32, projected.shape, 1)
    child = lax.broadcasted_iota(jnp.int32, projected.shape, 0) // (vectors.shape[0] // 2)
    outside = (position >= first).astype(jnp.int32)
    projected = jnp.where(outside == child, projected, 0.0)
    if with_sums:
        position = start + lax.broadcasted_iota(jnp.int32, (8, count), 1)
        which = lax.broadcasted_iota(jnp.int32, (8, count), 0)
        inside = (position < first).astype(F32)
        members = jnp.where(which == 0, inside, jnp.where(which == 1, 1.0 - inside, 0.0))
        projected = jnp.concatenate([projected, members], axis=0)
    return dot_split(split(projected), rows_split, PLAIN)


def factorize(grams):
    size = grams[0].shape[0]
    lane = lax.broadcasted_iota(jnp.int32, (size, size), 1)
    row = lax.broadcasted_iota(jnp.int32, (size, size), 0)
    eye = (lane == row).astype(F32)
    tables = [
        [jnp.concatenate([g, eye], axis=1)[t * 8 : t * 8 + 8] for t in range(size // 8)] for g in grams
    ]
    sub = lax.broadcasted_iota(jnp.int32, (8, 2 * size), 0)
    for step in range(size):
        tile, place = divmod(step, 8)
        for table in tables:
            pivot_row = table[tile][place : place + 1]
            pivot = pivot_row[:, step : step + 1]
            scaled = pivot_row / jnp.broadcast_to(pivot, pivot_row.shape)
            for t in range(tile, size // 8):
                column = jnp.broadcast_to(table[t][:, step : step + 1], table[t].shape)
                if t == tile:
                    column = jnp.where(sub > place, column, 0.0)
                table[t] = table[t] - column * scaled
    results = []
    for table in tables:
        full = jnp.concatenate(table, axis=0)
        upper, lower_inverse = full[:, :size], full[:, size:]
        diagonal = jnp.sum(jnp.where(lane == row, upper, 0.0), axis=1, keepdims=True)
        scale = 1.0 / jnp.sqrt(diagonal)
        results.append((jnp.where(lane >= row, upper * scale, 0.0), lower_inverse * scale))
    return results


def image(sums, vectors, mean, total):
    high, low = split(vectors)
    projected_mean = jnp.sum((high.astype(F32) + low.astype(F32)) * mean, axis=1, keepdims=True)
    return (sums - total * projected_mean * mean) / total


def member_counts(info, first, rows):
    group = 2 * first.shape[0] // CHILDREN
    base = info[CLUSTER] * group
    total = lax.fori_loop(0, group, lambda i, t: t + first[base + i], jnp.int32(0))
    return total.astype(F32), (group * rows - total).astype(F32)


def spans(info, first, rows):
    own, partner, upper = first[info[FLAT]], first[info[PARTNER]], info[UPPER] == 1
    return (
        jnp.where(upper, own, 0), jnp.where(upper, rows - own, own),
        jnp.where(upper, partner, 0), jnp.where(upper, rows - partner, partner),
    )


def column_blocks(info):
    for r in range(4):
        for far, c in ((False, info[CORE_AT]), (True, 1 - info[CORE_AT])):
            yield r, far, pl.ds(pl.multiple_of((c * 4 + (info[X_AT] ^ r)) * 128, 128), 128)


def first_kernel(info, first, basis_ref, rows_ref, mine_ref, other_ref, total):
    step = pl.program_id(0)
    count = rows_ref.shape[0]

    @pl.when(step == 0)
    def _():
        total[...] = jnp.zeros_like(total)

    own_first = first[info[FLAT]]
    total[...] += masked_products(basis_ref[...], rows_ref[...], own_first, step * count, True)

    @pl.when(step == pl.num_programs(0) - 1)
    def _():
        for r, far, columns in column_blocks(info):
            (other_ref if far else mine_ref)[r] = total[:, columns]


def middle_kernel(
    info, first, own_ref, far_ref, basis_ref, rows_ref,
    mine_ref, other_ref, vectors_ref, mean_ref, total, current, later,
):
    step = pl.program_id(0)
    count = rows_ref.shape[0]
    k = basis_ref.shape[0] // 2
    upper = info[UPPER]

    @pl.when(step == 0)
    def _():
        for r, far, columns in column_blocks(info):
            total[:, columns] = (far_ref if far else own_ref)[r]
        counts = member_counts(info, first, pl.num_programs(0) * count)
        images, grams = [], []
        for c in range(2):
            mean = total[2 * k + c : 2 * k + c + 1, :] / counts[c]
            mean_ref[pl.ds(c, 1), :] = mean
            images.append(image(total[c * k : c * k + k, :], basis_ref[c * k : c * k + k, :], mean, counts[c]))
            grams.append(dot_precise(images[c], images[c], ROW_BY_ROW))
        for c, (_, inverse) in enumerate(factorize(grams)):
            current[c * k : c * k + k, :] = dot_precise(inverse, images[c], PLAIN)
        vectors_ref[...] = current[pl.ds(pl.multiple_of(upper * k, k), k), :]
        later[...] = jnp.zeros_like(later)

    own_first = first[info[FLAT]]
    later[...] += masked_products(current[...], rows_ref[...], own_first, step * count, False)

    @pl.when(step == pl.num_programs(0) - 1)
    def _():
        for r, far, columns in column_blocks(info):
            for n, half in enumerate((upper, 1 - upper)):
                ref = other_ref if far else mine_ref
                ref[r, n * k : n * k + k] = later[pl.ds(pl.multiple_of(half * k, k), k), columns]


def last_kernel(info, first, own_ref, far_ref, vectors_ref, mean_ref, basis_ref, factor_ref, total, lower, *, rows):
    for r, far, columns in column_blocks(info):
        total[:, columns] = (far_ref if far else own_ref)[r]
    counts = member_counts(info, first, rows)
    child = info[UPPER]
    mean = jnp.where(child == 0, mean_ref[0:1, :], mean_ref[1:2, :])
    count = jnp.where(child == 0, counts[0], counts[1])
    image_rows = image(total[...], vectors_ref[...], mean, count)
    gram = dot_precise(image_rows, image_rows, ROW_BY_ROW)
    ((transposed, inverse),) = factorize([gram])
    total[...] = dot_precise(inverse, image_rows, PLAIN)
    lower[...] = transposed.T
    start = pl.multiple_of(info[PIECE], 8)
    basis_ref[...] = math.sqrt(total.shape[1]) * total[pl.ds(start, 8), :]
    factor_ref[...] = lower[pl.ds(start, 8), :]


def add_kernel(left_ref, right_ref, *outs):
    for r, out in enumerate(outs):
        out[...] = left_ref[r] + right_ref[r]


def shifted_rows(ref, start, count):
    aligned = pl.multiple_of(start // 8 * 8, 8)
    window = ref[pl.ds(aligned, count + 8), :]
    return pltpu.roll(window, jnp.where(start == aligned, 0, count + 8 - (start - aligned)), 0)[:count]


def piece_base(info, at, size, rows):
    return pl.multiple_of(jnp.where(info[UPPER] == 1, rows - at - size, at), 8)


def place_kernel(info, first, own_ref, *refs):
    pieces, out_ref, own, other, sems = refs[:-4], refs[-4], refs[-3], refs[-2], refs[-1]
    step = pl.program_id(0)
    count = out_ref.shape[0]
    rows = own_ref.shape[0]
    copies = [pltpu.make_async_copy(own_ref, own.at[pl.ds(0, rows)], sems.at[0])]
    at = 0
    for n, piece in enumerate(pieces):
        size = piece.shape[0]
        target = other.at[pl.ds(count + piece_base(info, at, size, rows), size)]
        copies.append(pltpu.make_async_copy(piece, target, sems.at[n + 1]))
        at += size

    @pl.when(step == 0)
    def _():
        for copy in copies:
            copy.start()
        for copy in copies:
            copy.wait()

    own_start, own_length, start, length = spans(info, first, rows)
    base = step * count
    place = base + lax.broadcasted_iota(jnp.int32, out_ref.shape, 0)
    own_rows = shifted_rows(own, jnp.minimum(own_start + base, rows), count)
    other_from = jnp.clip(base - own_length + start + count, 0, rows + count)
    other_rows = shifted_rows(other, other_from, count)
    there = place - own_length + start
    sent_from = jnp.where(info[UPPER] == 1, rows - SENT, 0)
    arrived = (there >= jnp.maximum(start, sent_from)) & (there < jnp.minimum(start + length, sent_from + SENT))
    out_ref[...] = jnp.where(place < own_length, own_rows, jnp.where(arrived, other_rows, 0.0))


def tail_kernel(info, first, piece_ref, moved_ref, out_ref, piece, window, edges, sems, *, at, rows, to):
    del moved_ref
    size = piece_ref.shape[0]
    _, own_length, start, length = spans(info, first, rows)
    base = piece_base(info, at, size, rows)
    low = jnp.maximum(base, start)
    count = jnp.minimum(base + size, start + length) - low
    target = own_length + low - start

    reached = functools.reduce(jnp.logical_or, [info[UPPER] == half for half in to])

    @pl.when(reached & (count > 0))
    def _():
        aligned = pl.multiple_of(target // 8 * 8, 8)
        skip = target - aligned
        tiles = (skip + count + 7) // 8
        tail = pl.multiple_of((tiles - 1) * 8, 8)
        loads = [
            pltpu.make_async_copy(piece_ref, piece.at[pl.ds(8, size)], sems.at[0]),
            pltpu.make_async_copy(out_ref.at[pl.ds(aligned, 8)], edges.at[pl.ds(0, 8)], sems.at[1]),
            pltpu.make_async_copy(out_ref.at[pl.ds(aligned + tail, 8)], edges.at[pl.ds(8, 8)], sems.at[2]),
        ]
        for load in loads:
            load.start()
        for load in loads:
            load.wait()
        rows_in = window.shape[0]
        window[...] = shifted_rows(piece, low - base - skip + 8, rows_in)
        row = lax.broadcasted_iota(jnp.int32, (8, window.shape[1]), 0)
        window[0:8] = jnp.where(row < skip, edges[0:8], window[0:8])
        kept = window[pl.ds(tail, 8), :]
        window[pl.ds(tail, 8), :] = jnp.where(row + tail < skip + count, kept, edges[8:16])

        def store(tile):
            at_row = pl.multiple_of(tile * 8, 8)
            return pltpu.make_async_copy(
                window.at[pl.ds(at_row, 8)], out_ref.at[pl.ds(pl.multiple_of(aligned + at_row, 8), 8)], sems.at[3 + tile]
            )

        @pl.loop(0, tiles)
        def _(tile):
            store(tile).start()

        @pl.loop(0, tiles)
        def _(tile):
            store(tile).wait()


def flip(values, axis, bits):
    size = 4 if axis == ("xl", "xh") else {"z": Z, "core": CORE}[axis]
    return lax.ppermute(values, axis, [(i, i ^ bits) for i in range(size)])


def flip_x(values, r):
    return flip(values, ("xl", "xh"), (r & 1) * 2 + (r >> 1))


def params():
    return pltpu.CompilerParams(vmem_limit_bytes=VMEM_LIMIT)


def cheap():
    return pl.CostEstimate(flops=1024, bytes_accessed=1024, transcendentals=0)


VMEM = pl.BlockSpec(memory_space=pltpu.VMEM)
ANY = pl.BlockSpec(memory_space=pl.ANY)


def shape(*dims):
    return jax.ShapeDtypeStruct(dims, F32)


def whole(*dims):
    return pl.BlockSpec(dims, lambda i, info, first: (0,) * len(dims))


def call(kernel, name, grid, in_specs, out_specs, out_shape, scratch=(), aliases=None):
    return pl.pallas_call(
        kernel,
        grid_spec=pltpu.PrefetchScalarGridSpec(
            num_scalar_prefetch=2, grid=grid, in_specs=in_specs, out_specs=out_specs, scratch_shapes=scratch
        ),
        out_shape=out_shape,
        input_output_aliases=aliases or {},
        compiler_params=params(),
        cost_estimate=cheap(),
        name=name,
    )


def add_pieces(left, right):
    n = left.shape[0]
    return pl.pallas_call(
        add_kernel, out_shape=[shape(*left.shape[1:])] * n, in_specs=[VMEM, VMEM], out_specs=[VMEM] * n,
        cost_estimate=cheap(), name="add_pieces",
    )(left, right)


def table_of_places():
    flat = np.arange(Y * Z * XL * XH * CORE)
    core, xh, xl, z, y = flat % 2, flat // 2 % 2, flat // 4 % 2, flat // 8 % Z, flat // (8 * Z)
    half = (Z // 2) * XL * XH * CORE
    piece = (z % (Z // 2) * XL + xl) * 8
    columns = [y, flat, flat ^ half, core, xh * 2 + xl, z // (Z // 2), piece, 0 * flat]
    return np.stack(columns, axis=1).astype(np.int32)


def body(embeddings, first_child, start_basis):
    rows, features = embeddings.shape
    k = start_basis.shape[0] // CHILDREN
    flat = lax.axis_index(AXES)
    info = lax.dynamic_slice_in_dim(jnp.asarray(table_of_places()), flat, 1, 0).reshape(-1)
    upper = lax.axis_index("z") // (Z // 2)
    barrier = lax.optimization_barrier

    edges = [sum(PIECES[:n]) for n in range(len(PIECES) + 1)]
    arrived = []

    def piece_of(source, at, size):
        start = jnp.where(upper == 1, at, rows - at - size)
        return lax.dynamic_slice_in_dim(source, start, size, 0)

    tails = [piece_of(embeddings, SENT, n * TAIL_ROWS) for n in range(1, TAIL + 1)]
    pieces = [piece_of(embeddings, a, b - a) for a, b in zip(edges[:-1], edges[1:])]

    def start_piece(after):
        piece, _ = barrier((pieces[len(arrived)], after))
        arrived.append(flip(piece, "z", Z // 2))

    def end_piece(n, *values):
        *values, arrived[n] = barrier((*values, arrived[n]))
        return values[0] if len(values) == 1 else values

    block = 256
    grid = (rows // block,)
    row_block = pl.BlockSpec((block, features), lambda i, info, first: (i, 0))
    basis_block = pl.BlockSpec((2 * k, features), lambda i, info, first: (info[0], 0))

    arrived.append(flip(pieces[0], "z", Z // 2))
    mine, other = call(
        first_kernel, "first_products", grid, [basis_block, row_block],
        [whole(4, 2 * k + 8, 128)] * 2, [shape(4, 2 * k + 8, 128)] * 2, [pltpu.VMEM((2 * k + 8, features), F32)],
    )(info, first_child, start_basis, embeddings)

    def scatter_x(parts):
        return parts[0] + flip_x(parts[1], 1) + flip_x(parts[2], 2) + flip_x(parts[3], 3)

    def sum_quad(total):
        return (total + flip(total, "z", 1)) + (flip(total, "z", 2) + flip(total, "z", 3))

    def gather_x(total):
        return jnp.stack([total] + [flip_x(total, r) for r in (1, 2, 3)])

    mine, other, pieces[1:], tails = barrier((mine, other, pieces[1:], tails))
    total = scatter_x(add_pieces(mine, flip(other, "core", 1)))
    total = sum_quad(end_piece(0, total + flip(total, "z", 4)))
    start_piece(total)
    own = gather_x(total)
    far = flip(own, "core", 1)
    mine, other, vectors, mean = call(
        middle_kernel, "middle", grid,
        [whole(4, 2 * k + 8, 128), whole(4, 2 * k + 8, 128), basis_block, row_block],
        [whole(4, 2 * k, 128), whole(4, 2 * k, 128), whole(k, features), whole(8, features)],
        [shape(4, 2 * k, 128)] * 2 + [shape(k, features), shape(8, features)],
        [pltpu.VMEM((2 * k + 8, features), F32), pltpu.VMEM((2 * k, features), F32), pltpu.VMEM((2 * k, features), F32)],
    )(info, first_child, own, far, start_basis, embeddings)

    total = scatter_x(add_pieces(mine, flip(other, "core", 1)))
    kept = sum_quad(end_piece(1, total[:k] + flip(total[k:], "z", 4)))
    start_piece(kept)
    own = gather_x(kept)
    far = flip(own, "core", 1)
    basis, factor = call(
        functools.partial(last_kernel, rows=rows), "last", (1,),
        [whole(4, k, 128), whole(4, k, 128), whole(k, features), whole(8, features)],
        [whole(8, features), whole(8, k)], [shape(8, features), shape(8, k)],
        [pltpu.VMEM((k, features), F32), pltpu.VMEM((k, k), F32)],
    )(info, first_child, own, far, vectors, mean)
    basis, factor = end_piece(2, basis, factor)

    out_block = 256

    def place(source, arrived):
        return call(
            place_kernel, "place", (2 * rows // out_block,), [ANY] * (1 + len(PIECES)),
            pl.BlockSpec((out_block, features), lambda i, info, first: (i, 0)), shape(2 * rows, features),
            [
                pltpu.VMEM((rows + out_block + 8, features), F32),
                pltpu.VMEM((rows + 2 * out_block + 8, features), F32),
                pltpu.SemaphoreType.DMA((1 + len(PIECES),)),
            ],
        )(info, first_child, source, *arrived)

    def place_tail(moved, piece, to):
        size = piece.shape[0]
        window = size + 16
        return call(
            functools.partial(tail_kernel, at=SENT, rows=rows, to=to), "place_tail", (1,), [ANY, ANY], ANY,
            shape(2 * rows, features),
            [
                pltpu.VMEM((size + 8 + window + 8, features), F32), pltpu.VMEM((window, features), F32),
                pltpu.VMEM((16, features), F32), pltpu.SemaphoreType.DMA((3 + window // 8,)),
            ],
            {3: 0},
        )(info, first_child, piece, moved)

    half = Z // 2

    def finish(up, down):
        upward = [(i, i + half) for i in range(half)]
        downward = [(i + half, i) for i in range(half)]

        def branch(source, tails, *arrived):
            sends = [(up, upward + downward, (0, 1))] if up == down else [(up, upward, (1,)), (down, downward, (0,))]
            got = [(lax.ppermute(tails[n - 1], "z", pairs), to) for n, pairs, to in sends if n]
            moved = place(source, arrived)
            for piece, to in got:
                moved = place_tail(moved, piece, to)
            return moved

        return branch

    def tail_pieces(needed):
        return (jnp.maximum(needed - SENT, 0) + TAIL_ROWS - 1) // TAIL_ROWS

    own_first, partner_first = first_child[flat], first_child[jnp.bitwise_xor(flat, half * XL * XH * CORE)]
    up = tail_pieces(rows - jnp.where(upper == 1, partner_first, own_first))
    down = tail_pieces(jnp.where(upper == 1, own_first, partner_first))
    branches = [finish(a, b) for a in range(TAIL + 1) for b in range(TAIL + 1)]
    moved_rows = lax.switch(up * (TAIL + 1) + down, branches, embeddings, tails, *arrived)
    return moved_rows, basis, factor


def solution(mesh):
    fine = Mesh(mesh.devices.reshape(Y, Z, XL, XH, CORE), AXES)
    return jax.shard_map(
        body,
        mesh=fine,
        in_specs=(P(AXES, None), P(), P()),
        out_specs=(P(AXES, None), P(("y", "z", "xl"), None), P(("y", "z", "xl"), None)),
        check_vma=False,
    )
```

```python
import functools
import math

import jax
import jax.numpy as jnp
import numpy as np
from jax import lax
from jax.experimental import pallas as pl
from jax.experimental.pallas import tpu as pltpu
from jax.sharding import Mesh, PartitionSpec as P

CHILDREN = 8
Y, Z, XL, XH, CORE = 4, 8, 2, 2, 2
AXES = ("y", "z", "xl", "xh", "core")
F32 = jnp.float32
VMEM_LIMIT = 40 * 1024 * 1024
PIECES = (216, 328, 224)
TAIL_ROWS = 128
TAIL = 2
SENT = sum(PIECES)
CLUSTER, FLAT, PARTNER, CORE_AT, X_AT, UPPER, PIECE = range(7)


def split(values):
    high = values.astype(jnp.bfloat16)
    return high, (values - high.astype(F32)).astype(jnp.bfloat16)


def dot_split(left, right, dims):
    (lh, ll), (rh, rl) = left, right

    def dot(a, b):
        return lax.dot_general(a, b, (dims, ((), ())), preferred_element_type=F32)

    return dot(lh, rh) + (dot(lh, rl) + dot(ll, rh))


ROW_BY_ROW = ((1,), (1,))
PLAIN = ((1,), (0,))


def dot_precise(left, right, dims):
    return lax.dot_general(
        left, right, (dims, ((), ())), precision=lax.Precision.HIGHEST, preferred_element_type=F32
    )


def masked_products(vectors, rows, first, start, with_sums):
    count = rows.shape[0]
    rows_split = split(rows)
    projected = dot_split(split(vectors), rows_split, ROW_BY_ROW)
    position = start + lax.broadcasted_iota(jnp.int32, projected.shape, 1)
    child = lax.broadcasted_iota(jnp.int32, projected.shape, 0) // (vectors.shape[0] // 2)
    outside = (position >= first).astype(jnp.int32)
    projected = jnp.where(outside == child, projected, 0.0)
    if with_sums:
        position = start + lax.broadcasted_iota(jnp.int32, (8, count), 1)
        which = lax.broadcasted_iota(jnp.int32, (8, count), 0)
        inside = (position < first).astype(F32)
        members = jnp.where(which == 0, inside, jnp.where(which == 1, 1.0 - inside, 0.0))
        projected = jnp.concatenate([projected, members], axis=0)
    return dot_split(split(projected), rows_split, PLAIN)


def factorize(grams):
    size = grams[0].shape[0]
    lane = lax.broadcasted_iota(jnp.int32, (size, size), 1)
    row = lax.broadcasted_iota(jnp.int32, (size, size), 0)
    eye = (lane == row).astype(F32)
    tables = [
        [jnp.concatenate([g, eye], axis=1)[t * 8 : t * 8 + 8] for t in range(size // 8)] for g in grams
    ]
    sub = lax.broadcasted_iota(jnp.int32, (8, 2 * size), 0)
    for step in range(size):
        tile, place = divmod(step, 8)
        for table in tables:
            pivot_row = table[tile][place : place + 1]
            pivot = pivot_row[:, step : step + 1]
            scaled = pivot_row / jnp.broadcast_to(pivot, pivot_row.shape)
            for t in range(tile, size // 8):
                column = jnp.broadcast_to(table[t][:, step : step + 1], table[t].shape)
                if t == tile:
                    column = jnp.where(sub > place, column, 0.0)
                table[t] = table[t] - column * scaled
    results = []
    for table in tables:
        full = jnp.concatenate(table, axis=0)
        upper, lower_inverse = full[:, :size], full[:, size:]
        diagonal = jnp.sum(jnp.where(lane == row, upper, 0.0), axis=1, keepdims=True)
        scale = 1.0 / jnp.sqrt(diagonal)
        results.append((jnp.where(lane >= row, upper * scale, 0.0), lower_inverse * scale))
    return results


def image(sums, vectors, mean, total):
    high, low = split(vectors)
    projected_mean = jnp.sum((high.astype(F32) + low.astype(F32)) * mean, axis=1, keepdims=True)
    return (sums - total * projected_mean * mean) / total


def member_counts(info, first, rows):
    group = 2 * first.shape[0] // CHILDREN
    base = info[CLUSTER] * group
    total = lax.fori_loop(0, group, lambda i, t: t + first[base + i], jnp.int32(0))
    return total.astype(F32), (group * rows - total).astype(F32)


def spans(info, first, rows):
    own, partner, upper = first[info[FLAT]], first[info[PARTNER]], info[UPPER] == 1
    return (
        jnp.where(upper, own, 0), jnp.where(upper, rows - own, own),
        jnp.where(upper, partner, 0), jnp.where(upper, rows - partner, partner),
    )


def column_blocks(info):
    for r in range(4):
        for far, c in ((False, info[CORE_AT]), (True, 1 - info[CORE_AT])):
            yield r, far, pl.ds(pl.multiple_of((c * 4 + (info[X_AT] ^ r)) * 128, 128), 128)


def first_kernel(info, first, basis_ref, rows_ref, mine_ref, other_ref, total):
    step = pl.program_id(0)
    count = rows_ref.shape[0]

    @pl.when(step == 0)
    def _():
        total[...] = jnp.zeros_like(total)

    own_first = first[info[FLAT]]
    total[...] += masked_products(basis_ref[...], rows_ref[...], own_first, step * count, True)

    @pl.when(step == pl.num_programs(0) - 1)
    def _():
        for r, far, columns in column_blocks(info):
            (other_ref if far else mine_ref)[r] = total[:, columns]


def middle_kernel(
    info, first, own_ref, far_ref, basis_ref, rows_ref,
    mine_ref, other_ref, vectors_ref, mean_ref, total, current, later,
):
    step = pl.program_id(0)
    count = rows_ref.shape[0]
    k = basis_ref.shape[0] // 2
    upper = info[UPPER]

    @pl.when(step == 0)
    def _():
        for r, far, columns in column_blocks(info):
            total[:, columns] = (far_ref if far else own_ref)[r]
        counts = member_counts(info, first, pl.num_programs(0) * count)
        images, grams = [], []
        for c in range(2):
            mean = total[2 * k + c : 2 * k + c + 1, :] / counts[c]
            mean_ref[pl.ds(c, 1), :] = mean
            images.append(image(total[c * k : c * k + k, :], basis_ref[c * k : c * k + k, :], mean, counts[c]))
            grams.append(dot_precise(images[c], images[c], ROW_BY_ROW))
        for c, (_, inverse) in enumerate(factorize(grams)):
            current[c * k : c * k + k, :] = dot_precise(inverse, images[c], PLAIN)
        vectors_ref[...] = current[pl.ds(pl.multiple_of(upper * k, k), k), :]
        later[...] = jnp.zeros_like(later)

    own_first = first[info[FLAT]]
    later[...] += masked_products(current[...], rows_ref[...], own_first, step * count, False)

    @pl.when(step == pl.num_programs(0) - 1)
    def _():
        for r, far, columns in column_blocks(info):
            for n, half in enumerate((upper, 1 - upper)):
                ref = other_ref if far else mine_ref
                ref[r, n * k : n * k + k] = later[pl.ds(pl.multiple_of(half * k, k), k), columns]


def last_kernel(info, first, own_ref, far_ref, vectors_ref, mean_ref, basis_ref, factor_ref, total, lower, *, rows):
    for r, far, columns in column_blocks(info):
        total[:, columns] = (far_ref if far else own_ref)[r]
    counts = member_counts(info, first, rows)
    child = info[UPPER]
    mean = jnp.where(child == 0, mean_ref[0:1, :], mean_ref[1:2, :])
    count = jnp.where(child == 0, counts[0], counts[1])
    image_rows = image(total[...], vectors_ref[...], mean, count)
    gram = dot_precise(image_rows, image_rows, ROW_BY_ROW)
    ((transposed, inverse),) = factorize([gram])
    total[...] = dot_precise(inverse, image_rows, PLAIN)
    lower[...] = transposed.T
    start = pl.multiple_of(info[PIECE], 8)
    basis_ref[...] = math.sqrt(total.shape[1]) * total[pl.ds(start, 8), :]
    factor_ref[...] = lower[pl.ds(start, 8), :]


def add_kernel(left_ref, right_ref, *outs):
    for r, out in enumerate(outs):
        out[...] = left_ref[r] + right_ref[r]


def shifted_rows(ref, start, count):
    aligned = pl.multiple_of(start // 8 * 8, 8)
    window = ref[pl.ds(aligned, count + 8), :]
    return pltpu.roll(window, jnp.where(start == aligned, 0, count + 8 - (start - aligned)), 0)[:count]


def piece_base(info, at, size, rows):
    return pl.multiple_of(jnp.where(info[UPPER] == 1, rows - at - size, at), 8)


def place_kernel(info, first, own_ref, *refs):
    pieces, out_ref, own, other, sems = refs[:-4], refs[-4], refs[-3], refs[-2], refs[-1]
    step = pl.program_id(0)
    count = out_ref.shape[0]
    rows = own_ref.shape[0]
    copies = [pltpu.make_async_copy(own_ref, own.at[pl.ds(0, rows)], sems.at[0])]
    at = 0
    for n, piece in enumerate(pieces):
        size = piece.shape[0]
        target = other.at[pl.ds(count + piece_base(info, at, size, rows), size)]
        copies.append(pltpu.make_async_copy(piece, target, sems.at[n + 1]))
        at += size

    @pl.when(step == 0)
    def _():
        for copy in copies:
            copy.start()
        for copy in copies:
            copy.wait()

    own_start, own_length, start, length = spans(info, first, rows)
    base = step * count
    place = base + lax.broadcasted_iota(jnp.int32, out_ref.shape, 0)
    own_rows = shifted_rows(own, jnp.minimum(own_start + base, rows), count)
    other_from = jnp.clip(base - own_length + start + count, 0, rows + count)
    other_rows = shifted_rows(other, other_from, count)
    there = place - own_length + start
    sent_from = jnp.where(info[UPPER] == 1, rows - SENT, 0)
    arrived = (there >= jnp.maximum(start, sent_from)) & (there < jnp.minimum(start + length, sent_from + SENT))
    out_ref[...] = jnp.where(place < own_length, own_rows, jnp.where(arrived, other_rows, 0.0))


def tail_kernel(info, first, piece_ref, moved_ref, out_ref, window, edges, sems, *, at, rows, to):
    del moved_ref
    size = piece_ref.shape[0]
    _, own_length, start, length = spans(info, first, rows)
    base = piece_base(info, at, size, rows)
    low = jnp.maximum(base, start)
    count = jnp.minimum(base + size, start + length) - low
    target = own_length + low - start
    reached = functools.reduce(jnp.logical_or, [info[UPPER] == half for half in to])

    @pl.when(reached & (count > 0))
    def _():
        aligned = pl.multiple_of(target // 8 * 8, 8)
        skip = target - aligned
        tiles = (skip + count + 7) // 8
        tail = pl.multiple_of((tiles - 1) * 8, 8)
        loads = [
            pltpu.make_async_copy(out_ref.at[pl.ds(aligned, 8)], edges.at[pl.ds(0, 8)], sems.at[0]),
            pltpu.make_async_copy(out_ref.at[pl.ds(aligned + tail, 8)], edges.at[pl.ds(8, 8)], sems.at[1]),
        ]
        for load in loads:
            load.start()
        rows_in = window.shape[0]
        offset = low - base - skip
        spare = jnp.zeros((rows_in - size, window.shape[1]), F32)
        shift = jnp.where(offset > 0, rows_in - offset, -offset)
        window[...] = pltpu.roll(jnp.concatenate([piece_ref[...], spare], axis=0), shift, 0)
        for load in loads:
            load.wait()
        row = lax.broadcasted_iota(jnp.int32, (8, window.shape[1]), 0)
        window[0:8] = jnp.where(row < skip, edges[0:8], window[0:8])
        kept = window[pl.ds(tail, 8), :]
        window[pl.ds(tail, 8), :] = jnp.where(row + tail < skip + count, kept, edges[8:16])

        def store(tile):
            at_row = pl.multiple_of(tile * 8, 8)
            return pltpu.make_async_copy(
                window.at[pl.ds(at_row, 8)], out_ref.at[pl.ds(pl.multiple_of(aligned + at_row, 8), 8)], sems.at[2 + tile]
            )

        @pl.loop(0, tiles)
        def _(tile):
            store(tile).start()

        @pl.loop(0, tiles)
        def _(tile):
            store(tile).wait()


def flip(values, axis, bits):
    size = 4 if axis == ("xl", "xh") else {"z": Z, "core": CORE}[axis]
    return lax.ppermute(values, axis, [(i, i ^ bits) for i in range(size)])


def flip_x(values, r):
    return flip(values, ("xl", "xh"), (r & 1) * 2 + (r >> 1))


def params():
    return pltpu.CompilerParams(vmem_limit_bytes=VMEM_LIMIT)


def cheap():
    return pl.CostEstimate(flops=1024, bytes_accessed=1024, transcendentals=0)


VMEM = pl.BlockSpec(memory_space=pltpu.VMEM)
ANY = pl.BlockSpec(memory_space=pl.ANY)


def shape(*dims):
    return jax.ShapeDtypeStruct(dims, F32)


def whole(*dims):
    return pl.BlockSpec(dims, lambda i, info, first: (0,) * len(dims))


def call(kernel, name, grid, in_specs, out_specs, out_shape, scratch=(), aliases=None):
    return pl.pallas_call(
        kernel,
        grid_spec=pltpu.PrefetchScalarGridSpec(
            num_scalar_prefetch=2, grid=grid, in_specs=in_specs, out_specs=out_specs, scratch_shapes=scratch
        ),
        out_shape=out_shape,
        input_output_aliases=aliases or {},
        compiler_params=params(),
        cost_estimate=cheap(),
        name=name,
    )


def add_pieces(left, right):
    n = left.shape[0]
    return pl.pallas_call(
        add_kernel, out_shape=[shape(*left.shape[1:])] * n, in_specs=[VMEM, VMEM], out_specs=[VMEM] * n,
        cost_estimate=cheap(), name="add_pieces",
    )(left, right)


def table_of_places():
    flat = np.arange(Y * Z * XL * XH * CORE)
    core, xh, xl, z, y = flat % 2, flat // 2 % 2, flat // 4 % 2, flat // 8 % Z, flat // (8 * Z)
    half = (Z // 2) * XL * XH * CORE
    piece = (z % (Z // 2) * XL + xl) * 8
    columns = [y, flat, flat ^ half, core, xh * 2 + xl, z // (Z // 2), piece, 0 * flat]
    return np.stack(columns, axis=1).astype(np.int32)


def body(embeddings, first_child, start_basis):
    rows, features = embeddings.shape
    k = start_basis.shape[0] // CHILDREN
    flat = lax.axis_index(AXES)
    info = lax.dynamic_slice_in_dim(jnp.asarray(table_of_places()), flat, 1, 0).reshape(-1)
    upper = lax.axis_index("z") // (Z // 2)
    barrier = lax.optimization_barrier

    edges = [sum(PIECES[:n]) for n in range(len(PIECES) + 1)]
    arrived = []

    def piece_of(source, at, size):
        start = jnp.where(upper == 1, at, rows - at - size)
        return lax.dynamic_slice_in_dim(source, start, size, 0)

    tails = [piece_of(embeddings, SENT, n * TAIL_ROWS) for n in range(1, TAIL + 1)]
    pieces = [piece_of(embeddings, a, b - a) for a, b in zip(edges[:-1], edges[1:])]

    def start_piece(after):
        piece, _ = barrier((pieces[len(arrived)], after))
        arrived.append(flip(piece, "z", Z // 2))

    def end_piece(n, *values):
        *values, arrived[n] = barrier((*values, arrived[n]))
        return values[0] if len(values) == 1 else values

    block = 256
    grid = (rows // block,)
    row_block = pl.BlockSpec((block, features), lambda i, info, first: (i, 0))
    basis_block = pl.BlockSpec((2 * k, features), lambda i, info, first: (info[0], 0))

    arrived.append(flip(pieces[0], "z", Z // 2))
    mine, other = call(
        first_kernel, "first_products", grid, [basis_block, row_block],
        [whole(4, 2 * k + 8, 128)] * 2, [shape(4, 2 * k + 8, 128)] * 2, [pltpu.VMEM((2 * k + 8, features), F32)],
    )(info, first_child, start_basis, embeddings)

    def scatter_x(parts):
        return parts[0] + flip_x(parts[1], 1) + flip_x(parts[2], 2) + flip_x(parts[3], 3)

    def sum_quad(total):
        return (total + flip(total, "z", 1)) + (flip(total, "z", 2) + flip(total, "z", 3))

    def gather_x(total):
        return jnp.stack([total] + [flip_x(total, r) for r in (1, 2, 3)])

    mine, other, pieces[1:], tails = barrier((mine, other, pieces[1:], tails))
    total = scatter_x(add_pieces(mine, flip(other, "core", 1)))
    total = sum_quad(end_piece(0, total + flip(total, "z", 4)))
    start_piece(total)
    own = gather_x(total)
    far = flip(own, "core", 1)
    mine, other, vectors, mean = call(
        middle_kernel, "middle", grid,
        [whole(4, 2 * k + 8, 128), whole(4, 2 * k + 8, 128), basis_block, row_block],
        [whole(4, 2 * k, 128), whole(4, 2 * k, 128), whole(k, features), whole(8, features)],
        [shape(4, 2 * k, 128)] * 2 + [shape(k, features), shape(8, features)],
        [pltpu.VMEM((2 * k + 8, features), F32), pltpu.VMEM((2 * k, features), F32), pltpu.VMEM((2 * k, features), F32)],
    )(info, first_child, own, far, start_basis, embeddings)

    total = scatter_x(add_pieces(mine, flip(other, "core", 1)))
    kept = sum_quad(end_piece(1, total[:k] + flip(total[k:], "z", 4)))
    start_piece(kept)
    own = gather_x(kept)
    far = flip(own, "core", 1)
    basis, factor = call(
        functools.partial(last_kernel, rows=rows), "last", (1,),
        [whole(4, k, 128), whole(4, k, 128), whole(k, features), whole(8, features)],
        [whole(8, features), whole(8, k)], [shape(8, features), shape(8, k)],
        [pltpu.VMEM((k, features), F32), pltpu.VMEM((k, k), F32)],
    )(info, first_child, own, far, vectors, mean)
    basis, factor = end_piece(2, basis, factor)

    out_block = 256

    def place(source, arrived):
        return call(
            place_kernel, "place", (2 * rows // out_block,), [ANY] * (1 + len(PIECES)),
            pl.BlockSpec((out_block, features), lambda i, info, first: (i, 0)), shape(2 * rows, features),
            [
                pltpu.VMEM((rows + out_block + 8, features), F32),
                pltpu.VMEM((rows + 2 * out_block + 8, features), F32),
                pltpu.SemaphoreType.DMA((1 + len(PIECES),)),
            ],
        )(info, first_child, source, *arrived)

    def place_tail(moved, piece, to):
        size = piece.shape[0]
        window = size + 16
        return call(
            functools.partial(tail_kernel, at=SENT, rows=rows, to=to), "place_tail", (1,), [VMEM, ANY], ANY,
            shape(2 * rows, features),
            [
                pltpu.VMEM((window, features), F32), pltpu.VMEM((16, features), F32),
                pltpu.SemaphoreType.DMA((2 + window // 8,)),
            ],
            {3: 0},
        )(info, first_child, piece, moved)

    half = Z // 2

    def finish(up, down):
        upward = [(i, i + half) for i in range(half)]
        downward = [(i + half, i) for i in range(half)]

        def branch(source, tails, *arrived):
            sends = [(up, upward + downward, (0, 1))] if up == down else [(up, upward, (1,)), (down, downward, (0,))]
            got = [(lax.ppermute(tails[n - 1], "z", pairs), to) for n, pairs, to in sends if n]
            moved = place(source, arrived)
            for piece, to in got:
                moved = place_tail(moved, piece, to)
            return moved

        return branch

    def tail_pieces(needed):
        return (jnp.maximum(needed - SENT, 0) + TAIL_ROWS - 1) // TAIL_ROWS

    own_first, partner_first = first_child[flat], first_child[jnp.bitwise_xor(flat, half * XL * XH * CORE)]
    up = tail_pieces(rows - jnp.where(upper == 1, partner_first, own_first))
    down = tail_pieces(jnp.where(upper == 1, own_first, partner_first))
    branches = [finish(a, b) for a in range(TAIL + 1) for b in range(TAIL + 1)]
    moved_rows = lax.switch(up * (TAIL + 1) + down, branches, embeddings, tails, *arrived)
    return moved_rows, basis, factor


def solution(mesh):
    fine = Mesh(mesh.devices.reshape(Y, Z, XL, XH, CORE), AXES)
    return jax.shard_map(
        body,
        mesh=fine,
        in_specs=(P(AXES, None), P(), P()),
        out_specs=(P(AXES, None), P(("y", "z", "xl"), None), P(("y", "z", "xl"), None)),
        check_vma=False,
    )
```

```python
import functools
import math

import jax
import jax.numpy as jnp
import numpy as np
from jax import lax
from jax.experimental import pallas as pl
from jax.experimental.pallas import tpu as pltpu
from jax.sharding import Mesh, PartitionSpec as P

CHILDREN = 8
Y, Z, XL, XH, CORE = 4, 8, 2, 2, 2
AXES = ("y", "z", "xl", "xh", "core")
F32 = jnp.float32
VMEM_LIMIT = 40 * 1024 * 1024
PIECES = (176, 328, 264)
TAIL_ROWS = 128
TAIL = 2
SENT = sum(PIECES)
CLUSTER, FLAT, PARTNER, CORE_AT, X_AT, UPPER, PIECE = range(7)


def split(values):
    high = values.astype(jnp.bfloat16)
    return high, (values - high.astype(F32)).astype(jnp.bfloat16)


def dot_split(left, right, dims):
    (lh, ll), (rh, rl) = left, right

    def dot(a, b):
        return lax.dot_general(a, b, (dims, ((), ())), preferred_element_type=F32)

    return dot(lh, rh) + (dot(lh, rl) + dot(ll, rh))


ROW_BY_ROW = ((1,), (1,))
PLAIN = ((1,), (0,))


def dot_precise(left, right, dims):
    return lax.dot_general(
        left, right, (dims, ((), ())), precision=lax.Precision.HIGHEST, preferred_element_type=F32
    )


def masked_products(vectors, rows, first, start, with_sums):
    count = rows.shape[0]
    rows_split = split(rows)
    projected = dot_split(split(vectors), rows_split, ROW_BY_ROW)
    position = start + lax.broadcasted_iota(jnp.int32, projected.shape, 1)
    child = lax.broadcasted_iota(jnp.int32, projected.shape, 0) // (vectors.shape[0] // 2)
    outside = (position >= first).astype(jnp.int32)
    projected = jnp.where(outside == child, projected, 0.0)
    if with_sums:
        position = start + lax.broadcasted_iota(jnp.int32, (8, count), 1)
        which = lax.broadcasted_iota(jnp.int32, (8, count), 0)
        inside = (position < first).astype(F32)
        members = jnp.where(which == 0, inside, jnp.where(which == 1, 1.0 - inside, 0.0))
        projected = jnp.concatenate([projected, members], axis=0)
    return dot_split(split(projected), rows_split, PLAIN)


def factorize(grams):
    size = grams[0].shape[0]
    lane = lax.broadcasted_iota(jnp.int32, (size, size), 1)
    row = lax.broadcasted_iota(jnp.int32, (size, size), 0)
    eye = (lane == row).astype(F32)
    tables = [
        [jnp.concatenate([g, eye], axis=1)[t * 8 : t * 8 + 8] for t in range(size // 8)] for g in grams
    ]
    sub = lax.broadcasted_iota(jnp.int32, (8, 2 * size), 0)
    for step in range(size):
        tile, place = divmod(step, 8)
        for table in tables:
            pivot_row = table[tile][place : place + 1]
            pivot = pivot_row[:, step : step + 1]
            scaled = pivot_row / jnp.broadcast_to(pivot, pivot_row.shape)
            for t in range(tile, size // 8):
                column = jnp.broadcast_to(table[t][:, step : step + 1], table[t].shape)
                if t == tile:
                    column = jnp.where(sub > place, column, 0.0)
                table[t] = table[t] - column * scaled
    results = []
    for table in tables:
        full = jnp.concatenate(table, axis=0)
        upper, lower_inverse = full[:, :size], full[:, size:]
        diagonal = jnp.sum(jnp.where(lane == row, upper, 0.0), axis=1, keepdims=True)
        scale = 1.0 / jnp.sqrt(diagonal)
        results.append((jnp.where(lane >= row, upper * scale, 0.0), lower_inverse * scale))
    return results


def image(sums, vectors, mean, total):
    high, low = split(vectors)
    projected_mean = jnp.sum((high.astype(F32) + low.astype(F32)) * mean, axis=1, keepdims=True)
    return (sums - total * projected_mean * mean) / total


def member_counts(info, first, rows):
    group = 2 * first.shape[0] // CHILDREN
    base = info[CLUSTER] * group
    total = lax.fori_loop(0, group, lambda i, t: t + first[base + i], jnp.int32(0))
    return total.astype(F32), (group * rows - total).astype(F32)


def spans(info, first, rows):
    own, partner, upper = first[info[FLAT]], first[info[PARTNER]], info[UPPER] == 1
    return (
        jnp.where(upper, own, 0), jnp.where(upper, rows - own, own),
        jnp.where(upper, partner, 0), jnp.where(upper, rows - partner, partner),
    )


def column_blocks(info):
    for r in range(4):
        for far, c in ((False, info[CORE_AT]), (True, 1 - info[CORE_AT])):
            yield r, far, pl.ds(pl.multiple_of((c * 4 + (info[X_AT] ^ r)) * 128, 128), 128)


def first_kernel(info, first, basis_ref, rows_ref, mine_ref, other_ref, total):
    step = pl.program_id(0)
    count = rows_ref.shape[0]

    @pl.when(step == 0)
    def _():
        total[...] = jnp.zeros_like(total)

    own_first = first[info[FLAT]]
    total[...] += masked_products(basis_ref[...], rows_ref[...], own_first, step * count, True)

    @pl.when(step == pl.num_programs(0) - 1)
    def _():
        for r, far, columns in column_blocks(info):
            (other_ref if far else mine_ref)[r] = total[:, columns]


def middle_kernel(
    info, first, own_ref, far_ref, basis_ref, rows_ref,
    mine_ref, other_ref, vectors_ref, mean_ref, total, current, later,
):
    step = pl.program_id(0)
    count = rows_ref.shape[0]
    k = basis_ref.shape[0] // 2
    upper = info[UPPER]

    @pl.when(step == 0)
    def _():
        for r, far, columns in column_blocks(info):
            total[:, columns] = (far_ref if far else own_ref)[r]
        counts = member_counts(info, first, pl.num_programs(0) * count)
        images, grams = [], []
        for c in range(2):
            mean = total[2 * k + c : 2 * k + c + 1, :] / counts[c]
            mean_ref[pl.ds(c, 1), :] = mean
            images.append(image(total[c * k : c * k + k, :], basis_ref[c * k : c * k + k, :], mean, counts[c]))
            grams.append(dot_precise(images[c], images[c], ROW_BY_ROW))
        for c, (_, inverse) in enumerate(factorize(grams)):
            current[c * k : c * k + k, :] = dot_precise(inverse, images[c], PLAIN)
        vectors_ref[...] = current[pl.ds(pl.multiple_of(upper * k, k), k), :]
        later[...] = jnp.zeros_like(later)

    own_first = first[info[FLAT]]
    later[...] += masked_products(current[...], rows_ref[...], own_first, step * count, False)

    @pl.when(step == pl.num_programs(0) - 1)
    def _():
        for r, far, columns in column_blocks(info):
            for n, half in enumerate((upper, 1 - upper)):
                ref = other_ref if far else mine_ref
                ref[r, n * k : n * k + k] = later[pl.ds(pl.multiple_of(half * k, k), k), columns]


def last_kernel(info, first, own_ref, far_ref, vectors_ref, mean_ref, basis_ref, factor_ref, total, lower, *, rows):
    for r, far, columns in column_blocks(info):
        total[:, columns] = (far_ref if far else own_ref)[r]
    counts = member_counts(info, first, rows)
    child = info[UPPER]
    mean = jnp.where(child == 0, mean_ref[0:1, :], mean_ref[1:2, :])
    count = jnp.where(child == 0, counts[0], counts[1])
    image_rows = image(total[...], vectors_ref[...], mean, count)
    gram = dot_precise(image_rows, image_rows, ROW_BY_ROW)
    ((transposed, inverse),) = factorize([gram])
    total[...] = dot_precise(inverse, image_rows, PLAIN)
    lower[...] = transposed.T
    start = pl.multiple_of(info[PIECE], 8)
    basis_ref[...] = math.sqrt(total.shape[1]) * total[pl.ds(start, 8), :]
    factor_ref[...] = lower[pl.ds(start, 8), :]


def add_kernel(left_ref, right_ref, *outs):
    for r, out in enumerate(outs):
        out[...] = left_ref[r] + right_ref[r]


def shifted_rows(ref, start, count):
    aligned = pl.multiple_of(start // 8 * 8, 8)
    window = ref[pl.ds(aligned, count + 8), :]
    return pltpu.roll(window, jnp.where(start == aligned, 0, count + 8 - (start - aligned)), 0)[:count]


def piece_base(info, at, size, rows):
    return pl.multiple_of(jnp.where(info[UPPER] == 1, rows - at - size, at), 8)


def place_kernel(info, first, own_ref, *refs):
    pieces, out_ref, own, other, sems = refs[:-4], refs[-4], refs[-3], refs[-2], refs[-1]
    step = pl.program_id(0)
    count = out_ref.shape[0]
    rows = own_ref.shape[0]
    copies = [pltpu.make_async_copy(own_ref, own.at[pl.ds(0, rows)], sems.at[0])]
    at = 0
    for n, piece in enumerate(pieces):
        size = piece.shape[0]
        target = other.at[pl.ds(count + piece_base(info, at, size, rows), size)]
        copies.append(pltpu.make_async_copy(piece, target, sems.at[n + 1]))
        at += size

    @pl.when(step == 0)
    def _():
        for copy in copies:
            copy.start()
        for copy in copies:
            copy.wait()

    own_start, own_length, start, length = spans(info, first, rows)
    base = step * count
    place = base + lax.broadcasted_iota(jnp.int32, out_ref.shape, 0)
    own_rows = shifted_rows(own, jnp.minimum(own_start + base, rows), count)
    other_from = jnp.clip(base - own_length + start + count, 0, rows + count)
    other_rows = shifted_rows(other, other_from, count)
    there = place - own_length + start
    sent_from = jnp.where(info[UPPER] == 1, rows - SENT, 0)
    arrived = (there >= jnp.maximum(start, sent_from)) & (there < jnp.minimum(start + length, sent_from + SENT))
    out_ref[...] = jnp.where(place < own_length, own_rows, jnp.where(arrived, other_rows, 0.0))


def tail_kernel(info, first, piece_ref, moved_ref, out_ref, window, edges, sems, *, at, rows, to):
    del moved_ref
    size = piece_ref.shape[0]
    _, own_length, start, length = spans(info, first, rows)
    base = piece_base(info, at, size, rows)
    low = jnp.maximum(base, start)
    count = jnp.minimum(base + size, start + length) - low
    target = own_length + low - start
    reached = functools.reduce(jnp.logical_or, [info[UPPER] == half for half in to])

    @pl.when(reached & (count > 0))
    def _():
        aligned = pl.multiple_of(target // 8 * 8, 8)
        skip = target - aligned
        tiles = (skip + count + 7) // 8
        tail = pl.multiple_of((tiles - 1) * 8, 8)
        loads = [
            pltpu.make_async_copy(out_ref.at[pl.ds(aligned, 8)], edges.at[pl.ds(0, 8)], sems.at[0]),
            pltpu.make_async_copy(out_ref.at[pl.ds(aligned + tail, 8)], edges.at[pl.ds(8, 8)], sems.at[1]),
        ]
        for load in loads:
            load.start()
        rows_in = window.shape[0]
        offset = low - base - skip
        spare = jnp.zeros((rows_in - size, window.shape[1]), F32)
        shift = jnp.where(offset > 0, rows_in - offset, -offset)
        window[...] = pltpu.roll(jnp.concatenate([piece_ref[...], spare], axis=0), shift, 0)
        for load in loads:
            load.wait()
        row = lax.broadcasted_iota(jnp.int32, (8, window.shape[1]), 0)
        window[0:8] = jnp.where(row < skip, edges[0:8], window[0:8])
        kept = window[pl.ds(tail, 8), :]
        window[pl.ds(tail, 8), :] = jnp.where(row + tail < skip + count, kept, edges[8:16])

        def store(tile):
            at_row = pl.multiple_of(tile * 8, 8)
            return pltpu.make_async_copy(
                window.at[pl.ds(at_row, 8)], out_ref.at[pl.ds(pl.multiple_of(aligned + at_row, 8), 8)], sems.at[2 + tile]
            )

        @pl.loop(0, tiles)
        def _(tile):
            store(tile).start()

        @pl.loop(0, tiles)
        def _(tile):
            store(tile).wait()


def flip(values, axis, bits):
    size = 4 if axis == ("xl", "xh") else {"z": Z, "core": CORE}[axis]
    return lax.ppermute(values, axis, [(i, i ^ bits) for i in range(size)])


def flip_x(values, r):
    return flip(values, ("xl", "xh"), (r & 1) * 2 + (r >> 1))


def params():
    return pltpu.CompilerParams(vmem_limit_bytes=VMEM_LIMIT)


def cheap():
    return pl.CostEstimate(flops=1024, bytes_accessed=1024, transcendentals=0)


VMEM = pl.BlockSpec(memory_space=pltpu.VMEM)
ANY = pl.BlockSpec(memory_space=pl.ANY)


def shape(*dims):
    return jax.ShapeDtypeStruct(dims, F32)


def whole(*dims):
    return pl.BlockSpec(dims, lambda i, info, first: (0,) * len(dims))


def call(kernel, name, grid, in_specs, out_specs, out_shape, scratch=(), aliases=None):
    return pl.pallas_call(
        kernel,
        grid_spec=pltpu.PrefetchScalarGridSpec(
            num_scalar_prefetch=2, grid=grid, in_specs=in_specs, out_specs=out_specs, scratch_shapes=scratch
        ),
        out_shape=out_shape,
        input_output_aliases=aliases or {},
        compiler_params=params(),
        cost_estimate=cheap(),
        name=name,
    )


def add_pieces(left, right):
    n = left.shape[0]
    return pl.pallas_call(
        add_kernel, out_shape=[shape(*left.shape[1:])] * n, in_specs=[VMEM, VMEM], out_specs=[VMEM] * n,
        cost_estimate=cheap(), name="add_pieces",
    )(left, right)


def table_of_places():
    flat = np.arange(Y * Z * XL * XH * CORE)
    core, xh, xl, z, y = flat % 2, flat // 2 % 2, flat // 4 % 2, flat // 8 % Z, flat // (8 * Z)
    half = (Z // 2) * XL * XH * CORE
    piece = (z % (Z // 2) * XL + xl) * 8
    columns = [y, flat, flat ^ half, core, xh * 2 + xl, z // (Z // 2), piece, 0 * flat]
    return np.stack(columns, axis=1).astype(np.int32)


def body(embeddings, first_child, start_basis):
    rows, features = embeddings.shape
    k = start_basis.shape[0] // CHILDREN
    flat = lax.axis_index(AXES)
    info = lax.dynamic_slice_in_dim(jnp.asarray(table_of_places()), flat, 1, 0).reshape(-1)
    upper = lax.axis_index("z") // (Z // 2)
    barrier = lax.optimization_barrier

    edges = [sum(PIECES[:n]) for n in range(len(PIECES) + 1)]
    arrived = []

    def piece_of(source, at, size):
        start = jnp.where(upper == 1, at, rows - at - size)
        return lax.dynamic_slice_in_dim(source, start, size, 0)

    tails = [piece_of(embeddings, SENT, n * TAIL_ROWS) for n in range(1, TAIL + 1)]
    pieces = [piece_of(embeddings, a, b - a) for a, b in zip(edges[:-1], edges[1:])]

    def start_piece(after):
        piece, _ = barrier((pieces[len(arrived)], after))
        arrived.append(flip(piece, "z", Z // 2))

    def end_piece(n, *values):
        *values, arrived[n] = barrier((*values, arrived[n]))
        return values[0] if len(values) == 1 else values

    block = 256
    grid = (rows // block,)
    row_block = pl.BlockSpec((block, features), lambda i, info, first: (i, 0))
    basis_block = pl.BlockSpec((2 * k, features), lambda i, info, first: (info[0], 0))

    arrived.append(flip(pieces[0], "z", Z // 2))
    mine, other = call(
        first_kernel, "first_products", grid, [basis_block, row_block],
        [whole(4, 2 * k + 8, 128)] * 2, [shape(4, 2 * k + 8, 128)] * 2, [pltpu.VMEM((2 * k + 8, features), F32)],
    )(info, first_child, start_basis, embeddings)

    def scatter_x(parts):
        return parts[0] + flip_x(parts[1], 1) + flip_x(parts[2], 2) + flip_x(parts[3], 3)

    def sum_quad(total):
        return (total + flip(total, "z", 1)) + (flip(total, "z", 2) + flip(total, "z", 3))

    def gather_x(total):
        return jnp.stack([total] + [flip_x(total, r) for r in (1, 2, 3)])

    mine, other, pieces[1:], tails = barrier((mine, other, pieces[1:], tails))
    total = scatter_x(add_pieces(mine, flip(other, "core", 1)))
    total = sum_quad(end_piece(0, total + flip(total, "z", 4)))
    start_piece(total)
    own = gather_x(total)
    far = flip(own, "core", 1)
    mine, other, vectors, mean = call(
        middle_kernel, "middle", grid,
        [whole(4, 2 * k + 8, 128), whole(4, 2 * k + 8, 128), basis_block, row_block],
        [whole(4, 2 * k, 128), whole(4, 2 * k, 128), whole(k, features), whole(8, features)],
        [shape(4, 2 * k, 128)] * 2 + [shape(k, features), shape(8, features)],
        [pltpu.VMEM((2 * k + 8, features), F32), pltpu.VMEM((2 * k, features), F32), pltpu.VMEM((2 * k, features), F32)],
    )(info, first_child, own, far, start_basis, embeddings)

    total = scatter_x(add_pieces(mine, flip(other, "core", 1)))
    kept = sum_quad(end_piece(1, total[:k] + flip(total[k:], "z", 4)))
    start_piece(kept)
    own = gather_x(kept)
    far = flip(own, "core", 1)
    basis, factor = call(
        functools.partial(last_kernel, rows=rows), "last", (1,),
        [whole(4, k, 128), whole(4, k, 128), whole(k, features), whole(8, features)],
        [whole(8, features), whole(8, k)], [shape(8, features), shape(8, k)],
        [pltpu.VMEM((k, features), F32), pltpu.VMEM((k, k), F32)],
    )(info, first_child, own, far, vectors, mean)
    basis, factor = end_piece(2, basis, factor)

    out_block = 256

    def place(source, arrived):
        return call(
            place_kernel, "place", (2 * rows // out_block,), [ANY] * (1 + len(PIECES)),
            pl.BlockSpec((out_block, features), lambda i, info, first: (i, 0)), shape(2 * rows, features),
            [
                pltpu.VMEM((rows + out_block + 8, features), F32),
                pltpu.VMEM((rows + 2 * out_block + 8, features), F32),
                pltpu.SemaphoreType.DMA((1 + len(PIECES),)),
            ],
        )(info, first_child, source, *arrived)

    def place_tail(moved, piece, to):
        size = piece.shape[0]
        window = size + 16
        return call(
            functools.partial(tail_kernel, at=SENT, rows=rows, to=to), "place_tail", (1,), [VMEM, ANY], ANY,
            shape(2 * rows, features),
            [
                pltpu.VMEM((window, features), F32), pltpu.VMEM((16, features), F32),
                pltpu.SemaphoreType.DMA((2 + window // 8,)),
            ],
            {3: 0},
        )(info, first_child, piece, moved)

    half = Z // 2

    def finish(up, down):
        upward = [(i, i + half) for i in range(half)]
        downward = [(i + half, i) for i in range(half)]

        def branch(source, tails, *arrived):
            sends = [(up, upward + downward, (0, 1))] if up == down else [(up, upward, (1,)), (down, downward, (0,))]
            got = [(lax.ppermute(tails[n - 1], "z", pairs), to) for n, pairs, to in sends if n]
            moved = place(source, arrived)
            for piece, to in got:
                moved = place_tail(moved, piece, to)
            return moved

        return branch

    def tail_pieces(needed):
        return (jnp.maximum(needed - SENT, 0) + TAIL_ROWS - 1) // TAIL_ROWS

    own_first, partner_first = first_child[flat], first_child[jnp.bitwise_xor(flat, half * XL * XH * CORE)]
    up = tail_pieces(rows - jnp.where(upper == 1, partner_first, own_first))
    down = tail_pieces(jnp.where(upper == 1, own_first, partner_first))
    branches = [finish(a, b) for a in range(TAIL + 1) for b in range(TAIL + 1)]
    moved_rows = lax.switch(up * (TAIL + 1) + down, branches, embeddings, tails, *arrived)
    return moved_rows, basis, factor


def solution(mesh):
    fine = Mesh(mesh.devices.reshape(Y, Z, XL, XH, CORE), AXES)
    return jax.shard_map(
        body,
        mesh=fine,
        in_specs=(P(AXES, None), P(), P()),
        out_specs=(P(AXES, None), P(("y", "z", "xl"), None), P(("y", "z", "xl"), None)),
        check_vma=False,
    )
```
